32 devices in a mesh: ctx: 8 (over z, x), wsh: 4 (over y, core).
Axes of the slice: x: 2, y: 2, z: 4, core: 2. Of those that a mesh axis runs over, the one named last changes fastest.
Arguments:
- tokens: bfloat16 [16, 2048, 768], P('wsh', 'ctx'), may hold values from -6 to 6
- doc_begin: int32 [16, 8], P('wsh', 'ctx'), may hold values from 0 to 4, as said below
- gain_attn: bfloat16 [768], P('wsh'), may hold values from 0.099609375 to 1.8984375
- w_qkv: bfloat16 [768, 2304], P('wsh'), may hold values from -0.21875 to 0.21875
- w_att_out: bfloat16 [768, 768], P('wsh'), may hold values from -1.75 to 1.75
- gain_mlp: bfloat16 [768], P('wsh'), may hold values from 0.099609375 to 1.8984375
- w_in: bfloat16 [768, 2304], P('wsh'), may hold values from -0.21875 to 0.21875
- w_down: bfloat16 [1152, 768], P('wsh'), may hold values from -0.1875 to 0.1875
- cotangent: bfloat16 [16, 2048, 768], P('wsh', 'ctx'), may hold values from -6 to 6
Outputs:
- output: bfloat16 [16, 2048, 768], P('wsh', 'ctx')
- grad_tokens: bfloat16 [16, 2048, 768], P('wsh', 'ctx')
- grad_gain_attn: float32 [768], P('wsh')
- grad_w_qkv: float32 [768, 2304], P('wsh')
- grad_w_att_out: float32 [768, 768], P('wsh')
- grad_gain_mlp: float32 [768], P('wsh')
- grad_w_in: float32 [768, 2304], P('wsh')
- grad_w_down: float32 [1152, 768], P('wsh')
The draws below stay inside these ranges and needn't reach their ends.
Inputs may be any that keep to these rules, and one draw needn't show every extreme that they name: `doc_begin`: never above the block's own index along the pack; every document begins at a block whose index is a multiple of 4 and holds 1024 tokens or more; of the 4 packs that share an index of wsh, one is a single document.
All inputs are finite; a program needn't handle non-finite values.
Results may differ from the reference program's by a relative error of at most 0.015.
Values may be sent and summed in bfloat16 or wider, within the bound.
No kernel may reach another device: no remote copies, remote signals or barrier semaphores. Data moves between devices by JAX's collectives and lax.ppermute only.
A program may use at most 192 MiB of HBM per device.

```python
import math
import jax
import jax.numpy as jnp
from jax import lax

D = 768
HEADS = 12
HEAD = 64
FF = 1152
HALF = 64
DOC_MIN = 1024
BLK = 256
PACK_DEV = 4
PACKS = 16
SPAN = 2048
N_CTX = 8
N_WSH = 4


def draw_doc_begin(key, part):
    key = jax.random.fold_in(key, 11)
    cut_key, pack_key, forced_key = jax.random.split(key, 3)
    stride_blocks = DOC_MIN // BLK
    blocks = jnp.arange(N_CTX, dtype=jnp.int32)
    allowed = (blocks % stride_blocks == 0) & (blocks > 0) & (blocks <= N_CTX - stride_blocks)
    tosses = jax.random.randint(cut_key, (PACKS, N_CTX), 0, 3)
    chosen = jax.random.randint(pack_key, (N_WSH, 1), 0, PACK_DEV)
    places = N_CTX // stride_blocks - 1
    forced_at = jax.random.randint(forced_key, (N_WSH, 1), 1, places + 1) * stride_blocks
    pack_of = (jnp.arange(PACKS, dtype=jnp.int32) % PACK_DEV).reshape(N_WSH, PACK_DEV)
    whole_pack = (pack_of == chosen).reshape(PACKS, 1)
    forced_pack = pack_of == (chosen + 1) % PACK_DEV
    forced_cut = (forced_pack[:, :, None] & (blocks[None, None, :] == forced_at[:, :, None])).reshape(PACKS, N_CTX)
    cut_here = allowed[None, :] & (tosses == 0) & jnp.logical_not(whole_pack) | forced_cut
    begins = jnp.where(cut_here, blocks[None, :], 0).astype(jnp.int32)
    return lax.cummax(begins, axis=1).astype(jnp.int32)


def levels(own_key, dims, pieces, least, high):
    def one(axis_at, blocks):
        heights = jax.random.uniform(jax.random.fold_in(jax.random.fold_in(own_key, 6), axis_at), (blocks,), jnp.float32, least / len(pieces), high / len(pieces))
        return jnp.repeat(jnp.exp(heights), dims[axis_at] // blocks).reshape((-1,) + (1,) * (len(dims) - axis_at - 1))

    level = one(*pieces[0])
    for cut in pieces[1:]:
        level = level * one(*cut)
    return level


def gaussian(key, dims, scale, reach, cuts=(), held_as=jnp.bfloat16):
    drawn = scale * jax.random.normal(key, dims, jnp.float32)
    if cuts:
        drawn = drawn * levels(key, dims, cuts, -0.22, 0.18)
    return jnp.clip(drawn, -reach, reach).astype(held_as)


def setup_inputs(seed: int = 0) -> dict:
    keys = jax.random.split(jax.random.key(seed), 10)
    return {
        "tokens": gaussian(keys[0], (PACKS, SPAN, D), 1.0, 6.0, ((0, 4), (1, 8))),
        "doc_begin": draw_doc_begin(jax.random.fold_in(keys[9], 71), 0),
        "gain_attn": jnp.clip(1.0 + 0.18 * jax.random.normal(keys[2], (D,), jnp.float32), 0.099609375, 1.8984375).astype(jnp.bfloat16),
        "w_qkv": gaussian(keys[3], (D, 3 * D), D ** -0.5, 0.21875, ((0, 4),)),
        "w_att_out": gaussian(keys[4], (D, D), (max(D // 64, 1)) ** -0.5, 1.75, ((0, 4),)),
        "gain_mlp": jnp.clip(1.0 + 0.18 * jax.random.normal(keys[5], (D,), jnp.float32), 0.099609375, 1.8984375).astype(jnp.bfloat16),
        "w_in": gaussian(keys[6], (D, 2 * FF), D ** -0.5, 0.21875, ((0, 4),)),
        "w_down": gaussian(keys[7], (FF, D), FF ** -0.5, 0.1875, ((0, 4),)),
        "cotangent": gaussian(keys[8], (PACKS, SPAN, D), 1.0, 6.0, ((0, 4), (1, 8))),
    }


@jax.custom_vjp
def low(v):
    return lax.optimization_barrier(v.astype(jnp.bfloat16)).astype(jnp.float32)

@jax.custom_vjp
def low_back(v):
    return v

def low_keep(v):
    return (low(v), None)

def low_pass(kept, grad):
    return (grad,)

def back_keep(v):
    return (v, None)

def back_low(kept, grad):
    return (low(grad),)
low.defvjp(low_keep, low_pass)
low_back.defvjp(back_keep, back_low)
EPS = 1e-05
THETA = 10000.0
MASKED = -1e+30
HIGH = lax.Precision.HIGHEST

def matmul_high(left, right):
    return jnp.dot(left, right, precision=HIGH, preferred_element_type=jnp.float32)

def layer_norm(values, gain):
    average = lax.optimization_barrier(jnp.mean(values, axis=-1, keepdims=True))
    centred = values - average
    variance = lax.optimization_barrier(jnp.mean(centred * centred, axis=-1, keepdims=True))
    return centred * lax.rsqrt(variance + EPS) * gain

def rotary_tables(positions):
    half_size = HEAD // 2
    freqs = jnp.power(THETA, -jnp.arange(half_size, dtype=jnp.float32) * (2.0 / HEAD))
    angles = positions[:, None] * freqs[None, :]
    cosine = jnp.concatenate([jnp.cos(angles), jnp.cos(angles)], axis=-1)[:, None, :]
    sine_tab = jnp.concatenate([jnp.sin(angles), jnp.sin(angles)], axis=-1)[:, None, :]
    return (cosine, sine_tab)

def rotate(values, cosine, sine_tab):
    half_size = values.shape[-1] // 2
    turned = jnp.concatenate([-values[..., half_size:], values[..., :half_size]], axis=-1)
    return values * cosine + turned * sine_tab

def window_attention(queries, keys_all, values_all, doc_ids):
    span_len = queries.shape[0]
    rows_block = math.gcd(span_len, 512)
    key_pad = jnp.pad(keys_all, ((HALF, HALF), (0, 0), (0, 0)))
    value_pad = jnp.pad(values_all, ((HALF, HALF), (0, 0), (0, 0)))
    doc_pad = jnp.pad(doc_ids, (HALF, HALF), constant_values=-1)
    offsets = jnp.arange(rows_block + 2 * HALF)[None, :] - HALF - jnp.arange(rows_block)[:, None]
    near = jnp.abs(offsets) <= HALF
    score_scale = HEAD ** (-0.5)

    def one_block(start):
        block_q = lax.dynamic_slice_in_dim(queries, start, rows_block, 0)
        block_k = lax.dynamic_slice_in_dim(key_pad, start, rows_block + 2 * HALF, 0)
        block_v = lax.dynamic_slice_in_dim(value_pad, start, rows_block + 2 * HALF, 0)
        doc_q = lax.dynamic_slice_in_dim(doc_ids, start, rows_block, 0)
        doc_k = lax.dynamic_slice_in_dim(doc_pad, start, rows_block + 2 * HALF, 0)
        allowed = near & (doc_q[:, None] == doc_k[None, :])
        raw = jnp.einsum('qhd,khd->hqk', block_q, block_k, precision=HIGH) * score_scale
        scores = jnp.where(allowed[None], low_back(raw), MASKED)
        probs = low(jax.nn.softmax(scores, axis=-1))
        return jnp.einsum('hqk,khd->qhd', probs, block_v, precision=HIGH)
    starts = jnp.arange(span_len // rows_block, dtype=jnp.int32) * rows_block
    blocks_out = lax.map(jax.checkpoint(one_block), starts)
    return blocks_out.reshape(span_len, HEADS * HEAD)

def pack_forward(inputs, doc_ids, gain_one, w_qkv, w_att_out, gain_two, w_in, w_down):
    span_len = inputs.shape[0]
    first_in = low(layer_norm(inputs, gain_one))
    projected = low_back(matmul_high(first_in, w_qkv)).reshape(span_len, 3, HEADS, HEAD)
    positions = jnp.arange(span_len).astype(jnp.float32)
    cosine, sine_tab = rotary_tables(positions)
    queries = low(rotate(projected[:, 0], cosine, sine_tab))
    keys_all = low(rotate(projected[:, 1], cosine, sine_tab))
    values_all = low(projected[:, 2])
    attn_mixed = low_back(low(window_attention(queries, keys_all, values_all, doc_ids)))
    middle = inputs + low_back(matmul_high(attn_mixed, w_att_out))
    second_in = low(layer_norm(middle, gain_two))
    gate_up = low_back(matmul_high(second_in, w_in))
    hidden = low(jax.nn.gelu(gate_up[:, :FF], approximate=False) * gate_up[:, FF:])
    return middle + matmul_high(hidden, w_down)

def reference(tokens, doc_begin, gain_attn, w_qkv, w_att_out, gain_mlp, w_in, w_down, cotangent):
    weights = (gain_attn.astype(jnp.float32), w_qkv.astype(jnp.float32), w_att_out.astype(jnp.float32), gain_mlp.astype(jnp.float32), w_in.astype(jnp.float32), w_down.astype(jnp.float32))
    inputs_all = tokens.astype(jnp.float32)
    doc_all = jnp.repeat(doc_begin, BLK, axis=1).astype(jnp.int32)
    upstream_all = cotangent.astype(jnp.float32)

    def one_pack(totals, pack_item):
        inputs, doc_ids, upstream = pack_item

        def forward(values_in, gain_one, weight_qkv, weight_out, gain_two, weight_in, weight_down):
            return pack_forward(values_in, doc_ids, gain_one, weight_qkv, weight_out, gain_two, weight_in, weight_down)
        result, pullback = jax.vjp(forward, inputs, *weights)
        grads_all = pullback(upstream)
        totals = tuple((prior + extra for prior, extra in zip(totals, grads_all[1:])))
        return (totals, (result, grads_all[0]))
    start_totals = tuple((jnp.zeros(weight.shape, jnp.float32) for weight in weights))
    totals, (results, grad_inputs) = lax.scan(one_pack, start_totals, (inputs_all, doc_all, upstream_all))
    return (results.astype(jnp.bfloat16), grad_inputs.astype(jnp.bfloat16), totals[0], totals[1], totals[2], totals[3], totals[4], totals[5])
```

```python
import functools
import math

import jax
import jax.numpy as jnp
from jax import lax
from jax.experimental import pallas as pl
from jax.experimental.pallas import tpu as pltpu
from jax.sharding import PartitionSpec as P

HEAD = 64
HALF = 64
EPS = 1e-05
THETA = 10000.0
MASKED = -1e30
PAIR = 2 * HEAD
QROWS = 128
WIN = QROWS + 2 * HALF
VMEM_BYTES = 56 * 1024 * 1024

F32 = jnp.float32
BF16 = jnp.bfloat16


def dot_nn(left, right):
    return jnp.dot(left, right, preferred_element_type=F32)


def dot_nt(left, right):
    return lax.dot_general(left, right, (((1,), (1,)), ((), ())), preferred_element_type=F32)


def dot_tn(left, right):
    return lax.dot_general(left, right, (((0,), (0,)), ((), ())), preferred_element_type=F32)


def swap(value, axis, bit):
    peers = lax.axis_size(axis)
    return lax.ppermute(value, axis, [(i, i ^ bit) for i in range(peers)])


def shifted(value, axis, by):
    peers = lax.axis_size(axis)
    return lax.ppermute(value, axis, [(i, i + by) for i in range(peers) if 0 <= i + by < peers])


def tied(value, *after):
    return lax.optimization_barrier((value,) + after)[0]


def shards_of(shard):
    near = swap(shard, "wsh", 1)
    far = swap(shard, "wsh", 2)
    far_near = swap(far, "wsh", 1)
    return (shard, near, far, far_near)


def pick(value, index, axis=0):
    return lax.dynamic_index_in_dim(value, index, axis, keepdims=False)


def added(kept, *received):
    total = kept.astype(F32)
    for item in received:
        total = total + item.astype(F32)
    return total.astype(BF16)


def reduced(grad):
    me_w, me_c = lax.axis_index("wsh"), lax.axis_index("ctx")
    rows, cols = grad.shape[0] // 4, grad.shape[1]
    core, side = me_w % 2, me_w // 2
    quarters = grad.reshape(2, 2, rows, cols)
    got = swap(pick(quarters, 1 - core, 1), "wsh", 1)
    pair = added(pick(quarters, core, 1), got)
    got = swap(pick(pair, 1 - side), "wsh", 2)
    mine = added(pick(pair, side), got)
    if lax.axis_size("ctx") != 8:
        return lax.psum(mine.astype(F32), "ctx")
    at_x, at_z = me_c % 2, me_c // 2
    half = cols // 2
    halves = lambda index: lax.dynamic_slice_in_dim(mine, index * half, half, 1)
    got = swap(halves(1 - at_x), "ctx", 1)
    part = added(halves(at_x), got)
    chunk = rows // 4
    chunks = lambda index: lax.dynamic_slice_in_dim(part, index * chunk, chunk, 0)
    got = [swap(chunks(at_z ^ d), "ctx", 2 * d) for d in (1, 2, 3)]
    own = added(chunks(at_z), *got)
    whole = jnp.zeros((rows, half), BF16)
    whole = lax.dynamic_update_slice_in_dim(whole, own, at_z * chunk, 0)
    for d in (1, 2, 3):
        whole = lax.dynamic_update_slice_in_dim(whole, swap(own, "ctx", 2 * d), (at_z ^ d) * chunk, 0)
    other = swap(whole, "ctx", 1)
    low = jnp.where(at_x == 0, whole, other)
    high = jnp.where(at_x == 0, other, whole)
    return jnp.concatenate([low, high], axis=1).astype(F32)


def reduced_small(value):
    if lax.axis_size("ctx") != 8:
        return lax.psum(value, ("ctx", "wsh"))
    for axis, bit in (("wsh", 1), ("wsh", 2), ("ctx", 1), ("ctx", 2), ("ctx", 4)):
        value = value + swap(value, axis, bit)
    return value


def stage_weight(me, shards, scratch, sems):
    rows = shards[0].shape[0]
    return [
        pltpu.make_async_copy(
            shard, scratch.at[pl.ds(pl.multiple_of((me ^ k) * rows, rows), rows)], sems.at[k]
        )
        for k, shard in enumerate(shards)
    ]


def norm_of(values):
    average = jnp.mean(values, axis=-1, keepdims=True)
    centred = values - average
    inverse = lax.rsqrt(jnp.mean(centred * centred, axis=-1, keepdims=True) + EPS)
    return centred * inverse, inverse


def norm_back(incoming, normal, inverse, gain):
    scaled = incoming * gain
    return inverse * (
        scaled
        - jnp.mean(scaled, axis=-1, keepdims=True)
        - normal * jnp.mean(scaled * normal, axis=-1, keepdims=True)
    )


def head_lanes():
    lane = lax.broadcasted_iota(jnp.int32, (1, PAIR), 1)
    return lane, lane < HEAD


def turned(value, lane):
    ahead = pltpu.roll(value, PAIR - HEAD // 2, 1)
    behind = pltpu.roll(value, HEAD // 2, 1)
    return jnp.where(lane % HEAD < HEAD // 2, ahead, behind)


def stacked(value, first, scale):
    one = jnp.where(first, scale, 0.0).astype(BF16)
    two = jnp.where(first, 0.0, scale).astype(BF16)
    return jnp.concatenate([value * one, value * two], axis=0)


def attend_kernel(
    me_ref, left_ok, right_ok, x_ref, hl_ref, hr_ref, gain_ref, cos_ref, sin_ref, s0, s1, s2, s3,
    q_ref, kv_ref, first_ref, probs_ref, mixed_ref, w_ref, sems,
):
    pack = pl.program_id(0)
    block = x_ref.shape[1]
    width = x_ref.shape[2]
    span = block + 2 * HALF

    @pl.when(pack == 0)
    def _():
        copies = stage_weight(me_ref[0], (s0, s1, s2, s3), w_ref, sems)
        for copy in copies:
            copy.start()
        for copy in copies:
            copy.wait()

    values = jnp.concatenate([hl_ref[0], x_ref[0], hr_ref[0]], axis=0).astype(F32)
    normal, _ = norm_of(values)
    first_ref[0] = (normal * gain_ref[...]).astype(BF16)
    lane, first = head_lanes()
    cos, sin = cos_ref[...], sin_ref[...]
    own = slice(HALF, HALF + block)
    step = 2 * PAIR
    for j in range(width // step):
        cols = slice(j * step, (j + 1) * step)
        q = dot_nn(first_ref[0, own, :], w_ref[:, cols])
        k = dot_nn(first_ref[0], w_ref[:, width + j * step : width + (j + 1) * step])
        v = dot_nn(first_ref[0], w_ref[:, 2 * width + j * step : 2 * width + (j + 1) * step])
        for i in range(2):
            part = slice(i * PAIR, (i + 1) * PAIR)
            base = j * step + i * PAIR
            qp, kp = q[:, part], k[:, part]
            q_ref[0, :, base : base + PAIR] = (
                qp * cos[own] + turned(qp, lane) * sin[own]
            ).astype(BF16)
            kv_ref[0, :, base : base + PAIR] = (kp * cos + turned(kp, lane) * sin).astype(BF16)
        kv_ref[0, :, width + j * step : width + (j + 1) * step] = v.astype(BF16)

    row = lax.broadcasted_iota(jnp.int32, (QROWS, WIN), 0)
    col = lax.broadcasted_iota(jnp.int32, (QROWS, WIN), 1)
    near = (col >= row) & (col <= row + 2 * HALF)
    blocks = block // QROWS
    for b in range(blocks):
        allowed = near
        if b == 0:
            allowed = allowed & ((col >= HALF) | (left_ok[pack] > 0))
        if b == blocks - 1:
            allowed = allowed & ((col < WIN - HALF) | (right_ok[pack] > 0))
        bias = jnp.where(allowed, 0.0, MASKED)
        bias = jnp.concatenate([bias, bias], axis=0)
        rows = slice(b * QROWS, (b + 1) * QROWS)
        window = slice(b * QROWS, b * QROWS + WIN)
        for p in range(width // PAIR):
            cols = slice(p * PAIR, (p + 1) * PAIR)
            q2 = stacked(q_ref[0, rows, cols], first, HEAD ** -0.5)
            scores = dot_nt(q2, kv_ref[0, window, cols]) + bias
            powers = jnp.exp(scores - jnp.max(scores, axis=-1, keepdims=True))
            probs = (powers * (1.0 / jnp.sum(powers, axis=-1, keepdims=True))).astype(BF16)
            probs_ref[0, p, b] = probs
            out = dot_nn(probs, kv_ref[0, window, width + p * PAIR : width + (p + 1) * PAIR])
            mixed_ref[0, rows, cols] = jnp.where(first, out[:QROWS], out[QROWS:]).astype(BF16)


def attention_forward(me, left_ok, right_ok, tokens, halo_left, halo_right, gain, cos, sin, shards):
    packs, block, width = tokens.shape
    span = block + 2 * HALF
    pairs, blocks = width // PAIR, block // QROWS
    per_pack = lambda *dims: pl.BlockSpec((1,) + dims, lambda i: (i,) + (0,) * len(dims))
    fixed = lambda *dims: pl.BlockSpec(dims, lambda i: (0,) * len(dims))
    smem = pl.BlockSpec(memory_space=pltpu.SMEM)
    return pl.pallas_call(
        attend_kernel,
        grid=(packs,),
        in_specs=[smem] * 3
        + [per_pack(block, width), per_pack(HALF, width), per_pack(HALF, width)]
        + [fixed(1, width), fixed(span, PAIR), fixed(span, PAIR)]
        + [pl.BlockSpec(memory_space=pl.ANY)] * 4,
        out_specs=[
            per_pack(block, width),
            per_pack(span, 2 * width),
            per_pack(span, width),
            per_pack(pairs, blocks, 2 * QROWS, WIN),
            per_pack(block, width),
        ],
        out_shape=[
            jax.ShapeDtypeStruct((packs, block, width), BF16),
            jax.ShapeDtypeStruct((packs, span, 2 * width), BF16),
            jax.ShapeDtypeStruct((packs, span, width), BF16),
            jax.ShapeDtypeStruct((packs, pairs, blocks, 2 * QROWS, WIN), BF16),
            jax.ShapeDtypeStruct((packs, block, width), BF16),
        ],
        scratch_shapes=[
            pltpu.VMEM((width, 3 * width), BF16),
            pltpu.SemaphoreType.DMA((4,)),
        ],
        compiler_params=pltpu.CompilerParams(vmem_limit_bytes=VMEM_BYTES),
        cost_estimate=pl.CostEstimate(flops=7_000_000_000, bytes_accessed=30_000_000, transcendentals=0),
        name="attend",
    )(me, left_ok, right_ok, tokens, halo_left, halo_right, gain, cos, sin, *shards)


def mlp_kernel(
    me_ref, x_ref, mixed_ref, up_ref, gain_ref, o0, o1, o2, o3, i0, i1, i2, i3, d0, d1, d2, d3,
    out_ref, second_ref, hidden_ref, ggu_ref, gm_ref, low_ref, gmix_ref, ggain_ref,
    wo_ref, wi_ref, wd_ref, sems,
):
    tile = pl.program_id(0)
    ff = wd_ref.shape[0]
    copies = [
        stage_weight(me_ref[0], group, scratch, sems.at[n])
        for n, (group, scratch) in enumerate(
            (((o0, o1, o2, o3), wo_ref), ((i0, i1, i2, i3), wi_ref), ((d0, d1, d2, d3), wd_ref))
        )
    ]

    @pl.when(tile == 0)
    def _():
        for group in copies:
            for copy in group:
                copy.start()
        ggain_ref[...] = jnp.zeros_like(ggain_ref)
        for group in copies:
            for copy in group:
                copy.wait()

    gain = gain_ref[...]
    middle = x_ref[0].astype(F32) + dot_nn(mixed_ref[0], wo_ref[...])
    normal, inverse = norm_of(middle)
    second = (normal * gain).astype(BF16)
    second_ref[0] = second
    upstream = up_ref[0]
    step = 384
    result = middle
    for j in range(ff // step):
        cols = slice(j * step, (j + 1) * step)
        ups = slice(ff + j * step, ff + (j + 1) * step)
        gate = dot_nn(second, wi_ref[:, cols])
        up = dot_nn(second, wi_ref[:, ups])
        grad_hidden = dot_nt(upstream, wd_ref[cols, :])
        cumulative = 0.5 + 0.5 * lax.erf(gate * (0.5 ** 0.5))
        activated = gate * cumulative
        density = jnp.exp(-0.5 * gate * gate) * (1.0 / math.sqrt(2.0 * math.pi))
        hidden = (activated * up).astype(BF16)
        hidden_ref[0, :, cols] = hidden
        ggu_ref[0, :, cols] = (grad_hidden * up * (cumulative + gate * density)).astype(BF16)
        ggu_ref[0, :, ups] = (grad_hidden * activated).astype(BF16)
        result = result + dot_nn(hidden, wd_ref[cols, :])
    out_ref[0] = result.astype(BF16)
    grad_second = dot_nt(ggu_ref[0], wi_ref[...])
    ggain_ref[...] += jnp.sum(grad_second * normal, axis=0, keepdims=True)
    grad_middle = upstream.astype(F32) + norm_back(grad_second, normal, inverse, gain)
    gm_ref[0] = grad_middle
    low = grad_middle.astype(BF16)
    low_ref[0] = low
    gmix_ref[0] = dot_nt(low, wo_ref[...]).astype(BF16)


def feed_forward(me, tokens, mixed, upstream, gain, out_shards, in_shards, down_shards):
    packs, block, width = tokens.shape
    ff = 4 * down_shards[0].shape[0]
    per_pack = lambda *dims: pl.BlockSpec((1,) + dims, lambda i: (i,) + (0,) * len(dims))
    fixed = lambda *dims: pl.BlockSpec(dims, lambda i: (0,) * len(dims))
    smem = pl.BlockSpec(memory_space=pltpu.SMEM)
    shape = lambda dtype, *dims: jax.ShapeDtypeStruct((packs, block) + dims, dtype)
    return pl.pallas_call(
        mlp_kernel,
        grid=(packs,),
        in_specs=[smem]
        + [per_pack(block, width)] * 3
        + [fixed(1, width)]
        + [pl.BlockSpec(memory_space=pl.ANY)] * 12,
        out_specs=[
            per_pack(block, width),
            per_pack(block, width),
            per_pack(block, ff),
            per_pack(block, 2 * ff),
            per_pack(block, width),
            per_pack(block, width),
            per_pack(block, width),
            fixed(1, width),
        ],
        out_shape=[
            shape(BF16, width),
            shape(BF16, width),
            shape(BF16, ff),
            shape(BF16, 2 * ff),
            shape(F32, width),
            shape(BF16, width),
            shape(BF16, width),
            jax.ShapeDtypeStruct((1, width), F32),
        ],
        scratch_shapes=[
            pltpu.VMEM((width, width), BF16),
            pltpu.VMEM((width, 2 * ff), BF16),
            pltpu.VMEM((ff, width), BF16),
            pltpu.SemaphoreType.DMA((3, 4)),
        ],
        compiler_params=pltpu.CompilerParams(vmem_limit_bytes=VMEM_BYTES),
        cost_estimate=pl.CostEstimate(flops=14_000_000_000, bytes_accessed=40_000_000, transcendentals=0),
        name="feed_forward",
    )(me, tokens, mixed, upstream, gain, *out_shards, *in_shards, *down_shards)


def attend_back_kernel(
    me_ref, q_ref, kv_ref, probs_ref, gmix_ref, x_ref, hl_ref, hr_ref, cos_ref, sin_ref,
    s0, s1, s2, s3,
    dq_ref, dkv_ref, own_ref, left_ref, right_ref, ggain_ref, w_ref, sems,
):
    pack = pl.program_id(0)
    block, width = q_ref.shape[1], q_ref.shape[2]
    span = block + 2 * HALF
    copies = stage_weight(me_ref[0], (s0, s1, s2, s3), w_ref, sems)

    @pl.when(pack == 0)
    def _():
        for copy in copies:
            copy.start()
        ggain_ref[...] = jnp.zeros_like(ggain_ref)
        for copy in copies:
            copy.wait()

    lane, first = head_lanes()
    cos, sin = cos_ref[...], -sin_ref[...]
    own = slice(HALF, HALF + block)
    blocks = block // QROWS
    for p in range(width // PAIR):
        cols = slice(p * PAIR, (p + 1) * PAIR)
        vcols = slice(width + p * PAIR, width + (p + 1) * PAIR)
        dqs, dks, dvs = [], [], []
        for b in range(blocks):
            rows = slice(b * QROWS, (b + 1) * QROWS)
            window = slice(b * QROWS, b * QROWS + WIN)
            q2 = stacked(q_ref[0, rows, cols], first, HEAD ** -0.5)
            do2 = stacked(gmix_ref[0, rows, cols], first, 1.0)
            probs = probs_ref[0, p, b]
            wide = probs.astype(F32)
            dprobs = dot_nt(do2, kv_ref[0, window, vcols])
            inner = jnp.sum(dprobs * wide, axis=-1, keepdims=True)
            ds = (wide * (dprobs - inner)).astype(BF16)
            dq2 = dot_nn(ds, kv_ref[0, window, cols])
            dqs.append(jnp.where(first, dq2[:QROWS], dq2[QROWS:]) * (HEAD ** -0.5))
            dks.append(dot_tn(ds, q2))
            dvs.append(dot_tn(probs, do2))
        dq = jnp.concatenate(dqs, axis=0)
        over = WIN - QROWS
        merge = lambda a, b: jnp.concatenate([a[:QROWS], a[QROWS:] + b[:over], b[over:]], axis=0)
        dk, dv = merge(*dks), merge(*dvs)
        dq_ref[0, :, cols] = (dq * cos[own] + turned(dq, lane) * sin[own]).astype(BF16)
        dkv_ref[0, :, cols] = (dk * cos + turned(dk, lane) * sin).astype(BF16)
        dkv_ref[0, :, vcols] = dv.astype(BF16)
    halo = dot_nt(dkv_ref[0], w_ref[:, width:])
    own_grad = halo[own] + dot_nt(dq_ref[0], w_ref[:, :width])
    own_ref[0] = own_grad
    left_ref[0] = halo[:HALF].astype(BF16)
    right_ref[0] = halo[HALF + block :].astype(BF16)
    values = jnp.concatenate([hl_ref[0], x_ref[0], hr_ref[0]], axis=0).astype(F32)
    normal, _ = norm_of(values)
    ggain_ref[...] += (
        jnp.sum(own_grad * normal[own], axis=0, keepdims=True)
        + jnp.sum(halo[:HALF] * normal[:HALF], axis=0, keepdims=True)
        + jnp.sum(halo[HALF + block :] * normal[HALF + block :], axis=0, keepdims=True)
    )


def attention_back(me, q, kv, probs, gmix, tokens, halo_left, halo_right, cos, sin, shards):
    packs, block, width = q.shape
    span = block + 2 * HALF
    pairs, blocks = width // PAIR, block // QROWS
    per_pack = lambda *dims: pl.BlockSpec((1,) + dims, lambda i: (i,) + (0,) * len(dims))
    fixed = lambda *dims: pl.BlockSpec(dims, lambda i: (0,) * len(dims))
    smem = pl.BlockSpec(memory_space=pltpu.SMEM)
    return pl.pallas_call(
        attend_back_kernel,
        grid=(packs,),
        in_specs=[
            smem,
            per_pack(block, width),
            per_pack(span, 2 * width),
            per_pack(pairs, blocks, 2 * QROWS, WIN),
            per_pack(block, width),
            per_pack(block, width),
            per_pack(HALF, width),
            per_pack(HALF, width),
            fixed(span, PAIR),
            fixed(span, PAIR),
        ]
        + [pl.BlockSpec(memory_space=pl.ANY)] * 4,
        out_specs=[
            per_pack(block, width),
            per_pack(span, 2 * width),
            per_pack(block, width),
            per_pack(HALF, width),
            per_pack(HALF, width),
            fixed(1, width),
        ],
        out_shape=[
            jax.ShapeDtypeStruct((packs, block, width), BF16),
            jax.ShapeDtypeStruct((packs, span, 2 * width), BF16),
            jax.ShapeDtypeStruct((packs, block, width), F32),
            jax.ShapeDtypeStruct((packs, HALF, width), BF16),
            jax.ShapeDtypeStruct((packs, HALF, width), BF16),
            jax.ShapeDtypeStruct((1, width), F32),
        ],
        scratch_shapes=[
            pltpu.VMEM((width, 3 * width), BF16),
            pltpu.SemaphoreType.DMA((4,)),
        ],
        compiler_params=pltpu.CompilerParams(vmem_limit_bytes=VMEM_BYTES),
        cost_estimate=pl.CostEstimate(flops=9_000_000_000, bytes_accessed=30_000_000, transcendentals=0),
        name="attend_back",
    )(me, q, kv, probs, gmix, tokens, halo_left, halo_right, cos, sin, *shards)


def finish_kernel(x_ref, own_ref, fl_ref, fr_ref, gm_ref, gain_ref, out_ref):
    block = x_ref.shape[1]
    normal, inverse = norm_of(x_ref[0].astype(F32))
    grad = own_ref[0]
    grad = jnp.concatenate(
        [
            grad[:HALF] + fl_ref[0].astype(F32),
            grad[HALF : block - HALF],
            grad[block - HALF :] + fr_ref[0].astype(F32),
        ],
        axis=0,
    )
    out_ref[0] = (gm_ref[0] + norm_back(grad, normal, inverse, gain_ref[...])).astype(BF16)


def finish(tokens, own, from_left, from_right, grad_middle, gain):
    packs, block, width = tokens.shape
    per_pack = lambda *dims: pl.BlockSpec((1,) + dims, lambda i: (i,) + (0,) * len(dims))
    return pl.pallas_call(
        finish_kernel,
        grid=(packs,),
        in_specs=[
            per_pack(block, width),
            per_pack(block, width),
            per_pack(HALF, width),
            per_pack(HALF, width),
            per_pack(block, width),
            pl.BlockSpec((1, width), lambda i: (0, 0)),
        ],
        out_specs=per_pack(block, width),
        out_shape=jax.ShapeDtypeStruct((packs, block, width), BF16),
        cost_estimate=pl.CostEstimate(flops=20_000_000, bytes_accessed=10_000_000, transcendentals=0),
        name="finish",
    )(tokens, own, from_left, from_right, grad_middle, gain)


def tables(start, count):
    half_size = HEAD // 2
    freqs = jnp.power(THETA, -jnp.arange(half_size, dtype=F32) * (2.0 / HEAD))
    positions = (start + jnp.arange(count, dtype=jnp.int32)).astype(F32)
    angles = positions[:, None] * freqs[None, :]
    cos, sin = jnp.cos(angles), jnp.sin(angles)
    return (
        jnp.concatenate([cos, cos, cos, cos], axis=-1),
        jnp.concatenate([-sin, sin, -sin, sin], axis=-1),
    )


def weight_grad(left, right):
    return dot_tn(
        left.reshape(-1, left.shape[-1]), right.reshape(-1, right.shape[-1])
    ).astype(BF16)


def per_device(tokens, doc_begin, gain_attn, w_qkv, w_att_out, gain_mlp, w_in, w_down, cotangent):
    packs, block, width = tokens.shape
    me_w, me_c = lax.axis_index("wsh"), lax.axis_index("ctx")
    me = me_w.reshape(1).astype(jnp.int32)

    gains = jnp.stack([gain_attn, gain_mlp])
    gain_parts = shards_of(gains)
    qkv_shards = shards_of(w_qkv)
    halo_left = shifted(tokens[:, block - HALF :], "ctx", 1)
    halo_right = shifted(tokens[:, :HALF], "ctx", -1)
    doc_right = shifted(doc_begin, "ctx", -1)
    gain_full = jnp.zeros((2, 4, gains.shape[1]), F32)
    for k, part in enumerate(gain_parts):
        gain_full = lax.dynamic_update_slice_in_dim(
            gain_full, part.astype(F32)[:, None], me_w ^ k, 1
        )
    gain_full = gain_full.reshape(2, width)
    gain_one, gain_two = gain_full[:1], gain_full[1:]
    left_ok = (doc_begin[:, 0] < me_c).astype(jnp.int32)
    right_ok = (
        (doc_right[:, 0] == doc_begin[:, 0]) & (me_c + 1 < lax.axis_size("ctx"))
    ).astype(jnp.int32)
    cos, sin = tables(me_c * block - HALF, block + 2 * HALF)

    out_shards = shards_of(tied(w_att_out, qkv_shards[2]))
    in_shards = shards_of(tied(w_in, out_shards[2]))
    down_shards = shards_of(tied(w_down, in_shards[2]))

    q, kv, first_in, probs, mixed = attention_forward(
        me, left_ok, right_ok, tokens, halo_left, halo_right, gain_one, cos, sin, qkv_shards
    )
    output, second_in, hidden, ggu, grad_middle, low, gmix, ggain_two = feed_forward(
        me, tokens, mixed, cotangent, gain_two, out_shards, in_shards, down_shards
    )
    grad_in = reduced(weight_grad(second_in, ggu))
    grad_down = reduced(weight_grad(hidden, cotangent))
    grad_out = reduced(weight_grad(mixed, low))
    dq, dkv, own, to_left, to_right, ggain_one = attention_back(
        me, q, kv, probs, gmix, tokens, halo_left, halo_right, cos, sin, qkv_shards
    )
    from_right = shifted(to_left, "ctx", -1)
    from_left = shifted(to_right, "ctx", 1)
    grad_qkv = reduced(
        jnp.concatenate(
            [weight_grad(first_in[:, HALF : HALF + block], dq), weight_grad(first_in, dkv)], axis=1
        )
    )
    grad_gains = reduced_small(jnp.concatenate([ggain_one, ggain_two], axis=0))
    grad_gains = lax.dynamic_slice_in_dim(grad_gains, me_w * gains.shape[1], gains.shape[1], 1)
    grad_tokens = finish(tokens, own, from_left, from_right, grad_middle, gain_one)
    return (
        output, grad_tokens, grad_gains[0], grad_qkv, grad_out, grad_gains[1], grad_in, grad_down,
    )


def solution(mesh):
    return jax.shard_map(
        per_device,
        mesh=mesh,
        in_specs=(
            P("wsh", "ctx", None),
            P("wsh", "ctx"),
            P("wsh"),
            P("wsh", None),
            P("wsh", None),
            P("wsh"),
            P("wsh", None),
            P("wsh", None),
            P("wsh", "ctx", None),
        ),
        out_specs=(
            P("wsh", "ctx", None),
            P("wsh", "ctx", None),
            P("wsh"),
            P("wsh", None),
            P("wsh", None),
            P("wsh"),
            P("wsh", None),
            P("wsh", None),
        ),
        check_vma=False,
    )
```

```python
import functools
import math

import jax
import jax.numpy as jnp
from jax import lax
from jax.experimental import pallas as pl
from jax.experimental.pallas import tpu as pltpu
from jax.sharding import PartitionSpec as P

HEAD = 64
HALF = 64
EPS = 1e-05
THETA = 10000.0
MASKED = -1e30
PAIR = 2 * HEAD
QROWS = 128
WIN = QROWS + 2 * HALF
VMEM_BYTES = 56 * 1024 * 1024
STEP = 1

F32 = jnp.float32
BF16 = jnp.bfloat16


def dot_nn(left, right):
    return jnp.dot(left, right, preferred_element_type=F32)


def dot_nt(left, right):
    return lax.dot_general(left, right, (((1,), (1,)), ((), ())), preferred_element_type=F32)


def dot_tn(left, right):
    return lax.dot_general(left, right, (((0,), (0,)), ((), ())), preferred_element_type=F32)


def swap(value, axis, bit):
    peers = lax.axis_size(axis)
    return lax.ppermute(value, axis, [(i, i ^ bit) for i in range(peers)])


def shifted(value, axis, by):
    peers = lax.axis_size(axis)
    return lax.ppermute(value, axis, [(i, i + by) for i in range(peers) if 0 <= i + by < peers])


def pick(value, index, axis=0):
    return lax.dynamic_index_in_dim(value, index, axis, keepdims=False)


def added(kept, *received):
    total = kept.astype(F32)
    for item in received:
        total = total + item.astype(F32)
    return total.astype(BF16)


class Reduction:
    def __init__(self, grad, bits=(1, 2)):
        self.bits = bits
        self.me_w, self.me_c = lax.axis_index("wsh"), lax.axis_index("ctx")
        self.at_first, self.at_second = (self.me_c // bit % 2 for bit in bits)
        self.value = grad.reshape(2, 2, grad.shape[0] // 4, grad.shape[1])
        self.small = lax.axis_size("ctx") == 8
        self.got = None

    def begin(self, send, axis, bit):
        self.got = swap(send, axis, bit)

    def begin_core(self):
        self.got = swap(pick(self.value, 1 - self.me_w % 2, 1), "wsh", 1)

    def end_core(self):
        self.value = added(pick(self.value, self.me_w % 2, 1), self.got)
        return self.value

    def join(self, other):
        self.value = jnp.concatenate([self.value, other.value], axis=1)

    def begin_side(self):
        self.begin(pick(self.value, 1 - self.me_w // 2), "wsh", 2)

    def end_side(self):
        self.value = added(pick(self.value, self.me_w // 2), self.got)
        self.half, self.chunk = self.value.shape[1] // 2, self.value.shape[0] // 2
        return self.value

    def halves(self, index):
        return lax.dynamic_slice_in_dim(self.value, index * self.half, self.half, 1)

    def chunks(self, index):
        return lax.dynamic_slice_in_dim(self.value, index * self.chunk, self.chunk, 0)

    def begin_across(self):
        self.got = None
        if self.small:
            self.begin(self.halves(1 - self.at_first), "ctx", self.bits[0])

    def end_across(self):
        if self.small:
            self.value = added(self.halves(self.at_first), self.got)
        return self.value

    def begin_near(self):
        self.got = None
        if self.small:
            self.begin(self.chunks(1 - self.at_second), "ctx", self.bits[1])

    def end_near(self):
        if self.small:
            self.value = added(self.chunks(self.at_second), self.got)
        return self.value

    def begin_far(self):
        self.got = None
        if self.small:
            self.begin(self.value, "ctx", 4)

    def end_far(self):
        if self.small:
            self.value = added(self.value, self.got)
        return self.value

    def begin_spread(self):
        self.got = None
        if self.small:
            self.begin(self.value, "ctx", self.bits[1])

    def end_spread(self):
        if self.small:
            self.value = joined(self.value, self.got, self.at_second, 0)
        return self.value

    def begin_last(self):
        self.got = None
        if self.small:
            self.begin(self.value, "ctx", self.bits[0])

    def end_last(self):
        if not self.small:
            return lax.psum(self.value.astype(F32), "ctx")
        return joined(self.value, self.got, self.at_first, 1).astype(F32)


def meet(sums, *arrays):
    sums = [item for item in sums if item.got is not None]
    out = lax.optimization_barrier(tuple(item.got for item in sums) + arrays)
    for item, got in zip(sums, out):
        item.got = got
    return out[len(sums) :]


def depart(*sums):
    for item, value in zip(sums, lax.optimization_barrier(tuple(item.value for item in sums))):
        item.value = value


def joined(mine, other, place, axis):
    low = jnp.where(place == 0, mine, other)
    high = jnp.where(place == 0, other, mine)
    return jnp.concatenate([low, high], axis=axis)


def stage_weight(me, shards, scratch, sems, start=0):
    rows = scratch.shape[0] // 4
    return [
        pltpu.make_async_copy(
            shard.at[pl.ds(start, rows)], scratch.at[pl.ds(pl.multiple_of((me ^ k) * rows, rows), rows)], sems.at[k]
        )
        for k, shard in enumerate(shards)
    ]


def norm_of(values):
    average = jnp.mean(values, axis=-1, keepdims=True)
    centred = values - average
    inverse = lax.rsqrt(jnp.mean(centred * centred, axis=-1, keepdims=True) + EPS)
    return centred * inverse, inverse


def norm_back(incoming, normal, inverse, gain):
    scaled = incoming * gain
    return inverse * (
        scaled
        - jnp.mean(scaled, axis=-1, keepdims=True)
        - normal * jnp.mean(scaled * normal, axis=-1, keepdims=True)
    )


def head_lanes():
    lane = lax.broadcasted_iota(jnp.int32, (1, PAIR), 1)
    return lane, lane < HEAD


def turned(value, lane):
    ahead = pltpu.roll(value, PAIR - HEAD // 2, 1)
    behind = pltpu.roll(value, HEAD // 2, 1)
    return jnp.where(lane % HEAD < HEAD // 2, ahead, behind)


def stacked(value, first, scale):
    one = jnp.where(first, scale, 0.0).astype(BF16)
    two = jnp.where(first, 0.0, scale).astype(BF16)
    return jnp.concatenate([value * one, value * two], axis=0)


def per_pack(*dims, packs=1):
    return pl.BlockSpec((packs,) + dims, lambda i: (i,) + (0,) * len(dims))


def rows_of(ref):
    return ref[...].reshape(-1, ref.shape[-1])


def put(ref, value):
    ref[...] = value.astype(ref.dtype).reshape(ref.shape)


def fixed(*dims):
    return pl.BlockSpec(dims, lambda i: (0,) * len(dims))


def cost(gflops, megabytes):
    return pl.CostEstimate(
        flops=int(gflops * 1e8), bytes_accessed=int(megabytes * 1e5), transcendentals=0
    )


def ordered(kernel, count, after):
    return lambda *refs: kernel(*refs[:count], *refs[count + len(after) :])


SMEM = pl.BlockSpec(memory_space=pltpu.SMEM)
ANY = pl.BlockSpec(memory_space=pl.ANY)
PARAMS = pltpu.CompilerParams(vmem_limit_bytes=VMEM_BYTES)


def project_kernel(
    me_ref, x_ref, hl_ref, hr_ref, cos_ref, sin_ref, s0, s1, s2, s3,
    q_ref, kv_ref, first_ref, w_ref, gain_ref, sems, gain_sems,
):
    pack = pl.program_id(0)
    block = x_ref.shape[1]
    width = x_ref.shape[2]
    shards = (s0, s1, s2, s3)
    copies = stage_weight(me_ref[0], shards, w_ref, sems)
    gains = [
        pltpu.make_async_copy(
            shard.at[pl.ds(width // 4, 16), pl.ds(0, width)], gain_ref.at[n], gain_sems.at[n]
        )
        for n, shard in enumerate(shards)
    ]

    @pl.when(pack == 0)
    def _():
        for copy in gains + copies:
            copy.start()
        for copy in gains:
            copy.wait()

    values = jnp.concatenate([hl_ref[0], x_ref[0], hr_ref[0]], axis=0).astype(F32)
    normal, _ = norm_of(values)
    gain = jnp.sum(gain_ref[...].astype(F32), axis=0)[:1]
    first_ref[0] = (normal * gain).astype(BF16)
    lane, first = head_lanes()
    cos, sin = cos_ref[...], sin_ref[...]
    own = slice(HALF, HALF + block)
    step = 2 * PAIR

    @pl.when(pack == 0)
    def _():
        for copy in copies:
            copy.wait()

    for j in range(width // step):
        cols = slice(j * step, (j + 1) * step)
        q = dot_nn(first_ref[0, own, :], w_ref[:, cols])
        k = dot_nn(first_ref[0], w_ref[:, width + j * step : width + (j + 1) * step])
        v = dot_nn(first_ref[0], w_ref[:, 2 * width + j * step : 2 * width + (j + 1) * step])
        for i in range(2):
            part = slice(i * PAIR, (i + 1) * PAIR)
            base = j * step + i * PAIR
            qp, kp = q[:, part], k[:, part]
            q_ref[0, :, base : base + PAIR] = (
                qp * cos[own] + turned(qp, lane) * sin[own]
            ).astype(BF16)
            kv_ref[0, :, base : base + PAIR] = (kp * cos + turned(kp, lane) * sin).astype(BF16)
        kv_ref[0, :, width + j * step : width + (j + 1) * step] = v.astype(BF16)


def project(me, tokens, halo_left, halo_right, cos, sin, shards):
    packs, block, width = tokens.shape
    span = block + 2 * HALF
    return pl.pallas_call(
        project_kernel,
        grid=(packs,),
        in_specs=[SMEM, per_pack(block, width), per_pack(HALF, width), per_pack(HALF, width)]
        + [fixed(span, PAIR), fixed(span, PAIR)]
        + [ANY] * 4,
        out_specs=[per_pack(block, width), per_pack(span, 2 * width), per_pack(span, width)],
        out_shape=[
            jax.ShapeDtypeStruct((packs, block, width), BF16),
            jax.ShapeDtypeStruct((packs, span, 2 * width), BF16),
            jax.ShapeDtypeStruct((packs, span, width), BF16),
        ],
        scratch_shapes=[
            pltpu.VMEM((width, 3 * width), BF16),
            pltpu.VMEM((4, 16, width), BF16),
            pltpu.SemaphoreType.DMA((4,)),
            pltpu.SemaphoreType.DMA((4,)),
        ],
        compiler_params=PARAMS,
        cost_estimate=cost(5, 15),
        name="project",
    )(me, tokens, halo_left, halo_right, cos, sin, *shards)


def attend_kernel(left_ok, right_ok, q_ref, kv_ref, probs_ref, mixed_ref):
    pack = pl.program_id(0)
    block, width = q_ref.shape[1], q_ref.shape[2]
    _, first = head_lanes()
    row = lax.broadcasted_iota(jnp.int32, (QROWS, WIN), 0)
    col = lax.broadcasted_iota(jnp.int32, (QROWS, WIN), 1)
    near = (col >= row) & (col <= row + 2 * HALF)
    blocks = block // QROWS
    for b in range(blocks):
        allowed = near
        if b == 0:
            allowed = allowed & ((col >= HALF) | (left_ok[pack] > 0))
        if b == blocks - 1:
            allowed = allowed & ((col < WIN - HALF) | (right_ok[pack] > 0))
        bias = jnp.where(allowed, 0.0, MASKED)
        bias = jnp.concatenate([bias, bias], axis=0)
        rows = slice(b * QROWS, (b + 1) * QROWS)
        window = slice(b * QROWS, b * QROWS + WIN)
        for p in range(width // PAIR):
            cols = slice(p * PAIR, (p + 1) * PAIR)
            q2 = stacked(q_ref[0, rows, cols], first, HEAD ** -0.5)
            scores = dot_nt(q2, kv_ref[0, window, cols]) + bias
            powers = jnp.exp(scores - jnp.max(scores, axis=-1, keepdims=True))
            probs = (powers * (1.0 / jnp.sum(powers, axis=-1, keepdims=True))).astype(BF16)
            probs_ref[0, p, b] = probs
            out = dot_nn(probs, kv_ref[0, window, width + p * PAIR : width + (p + 1) * PAIR])
            mixed_ref[0, rows, cols] = jnp.where(first, out[:QROWS], out[QROWS:]).astype(BF16)


def attend(after, left_ok, right_ok, q, kv):
    packs, block, width = q.shape
    pairs, blocks = width // PAIR, block // QROWS
    return pl.pallas_call(
        ordered(attend_kernel, 4, after),
        grid=(packs,),
        in_specs=[SMEM, SMEM, per_pack(block, width), per_pack(block + 2 * HALF, 2 * width)]
        + [ANY] * len(after),
        out_specs=[per_pack(pairs, blocks, 2 * QROWS, WIN), per_pack(block, width)],
        out_shape=[
            jax.ShapeDtypeStruct((packs, pairs, blocks, 2 * QROWS, WIN), BF16),
            jax.ShapeDtypeStruct((packs, block, width), BF16),
        ],
        compiler_params=PARAMS,
        cost_estimate=cost(10, 15),
        name="attend",
    )(left_ok, right_ok, q, kv, *after)


def hidden_kernel(
    me_ref, x_ref, mixed_ref, up_ref, gain_ref, o0, o1, o2, o3, i0, i1, i2, i3,
    out_ref, second_ref, hidden_ref, ggu_ref, middle_ref,
    wo_ref, wi_ref, wd_ref, sems,
):
    tile = pl.program_id(0)
    ff = wd_ref.shape[0]
    both = (o0, o1, o2, o3)
    copies = [
        stage_weight(me_ref[0], both, wo_ref, sems.at[0]),
        stage_weight(me_ref[0], (i0, i1, i2, i3), wi_ref, sems.at[1]),
        stage_weight(me_ref[0], both, wd_ref, sems.at[2], wo_ref.shape[0] // 4),
    ]

    @pl.when(tile == 0)
    def _():
        for group in copies:
            for copy in group:
                copy.start()
        for copy in copies[0]:
            copy.wait()

    middle = rows_of(x_ref).astype(F32) + dot_nn(rows_of(mixed_ref), wo_ref[...])
    put(middle_ref, middle)
    normal, _ = norm_of(middle)
    second = (normal * gain_ref[...]).astype(BF16)
    put(second_ref, second)
    upstream = rows_of(up_ref)

    @pl.when(tile == 0)
    def _():
        for group in copies[1:]:
            for copy in group:
                copy.wait()

    step = 384
    result = middle
    for j in range(ff // step):
        cols = slice(j * step, (j + 1) * step)
        ups = slice(ff + j * step, ff + (j + 1) * step)
        gate = dot_nn(second, wi_ref[:, cols])
        up = dot_nn(second, wi_ref[:, ups])
        grad_hidden = dot_nt(upstream, wd_ref[cols, :])
        cumulative = 0.5 + 0.5 * lax.erf(gate * (0.5 ** 0.5))
        activated = gate * cumulative
        density = jnp.exp(-0.5 * gate * gate) * (1.0 / math.sqrt(2.0 * math.pi))
        hidden = (activated * up).astype(BF16)
        put(hidden_ref.at[:, :, cols], hidden)
        put(ggu_ref.at[:, :, cols], grad_hidden * up * (cumulative + gate * density))
        put(ggu_ref.at[:, :, ups], grad_hidden * activated)
        result = result + dot_nn(hidden, wd_ref[cols, :])
    put(out_ref, result)


def hidden_layer(me, tokens, mixed, upstream, gain, both_shards, in_shards):
    packs, block, width = tokens.shape
    ff = in_shards[0].shape[1] // 2
    shape = lambda dtype, *dims: jax.ShapeDtypeStruct((packs, block) + dims, dtype)
    return pl.pallas_call(
        hidden_kernel,
        grid=(packs // STEP,),
        in_specs=[SMEM] + [per_pack(block, width, packs=STEP)] * 3 + [fixed(1, width)] + [ANY] * 8,
        out_specs=[
            per_pack(block, width, packs=STEP),
            per_pack(block, width, packs=STEP),
            per_pack(block, ff, packs=STEP),
            per_pack(block, 2 * ff, packs=STEP),
            per_pack(block, width, packs=STEP),
        ],
        out_shape=[
            shape(BF16, width),
            shape(BF16, width),
            shape(BF16, ff),
            shape(BF16, 2 * ff),
            shape(F32, width),
        ],
        scratch_shapes=[
            pltpu.VMEM((width, width), BF16),
            pltpu.VMEM((width, 2 * ff), BF16),
            pltpu.VMEM((ff, width), BF16),
            pltpu.SemaphoreType.DMA((3, 4)),
        ],
        compiler_params=PARAMS,
        cost_estimate=cost(16, 25),
        name="hidden_layer",
    )(me, tokens, mixed, upstream, gain, *both_shards, *in_shards)


def middle_kernel(
    me_ref, middle_ref, ggu_ref, up_ref, gain_ref, o0, o1, o2, o3, i0, i1, i2, i3,
    gm_ref, low_ref, gmix_ref, wo_ref, wi_ref, sems,
):
    tile = pl.program_id(0)
    copies = [
        stage_weight(me_ref[0], group, scratch, sems.at[n])
        for n, (group, scratch) in enumerate(
            (((o0, o1, o2, o3), wo_ref), ((i0, i1, i2, i3), wi_ref))
        )
    ]

    @pl.when(tile == 0)
    def _():
        for group in copies:
            for copy in group:
                copy.start()

    normal, inverse = norm_of(rows_of(middle_ref))

    @pl.when(tile == 0)
    def _():
        for group in copies:
            for copy in group:
                copy.wait()

    grad_second = dot_nt(rows_of(ggu_ref), wi_ref[...])
    grad_middle = rows_of(up_ref).astype(F32) + norm_back(grad_second, normal, inverse, gain_ref[...])
    put(gm_ref, grad_middle)
    low = grad_middle.astype(BF16)
    put(low_ref, low)
    put(gmix_ref, dot_nt(low, wo_ref[...]))


def middle_back(after, me, middle, ggu, upstream, gain, out_shards, in_shards):
    packs, block, width = middle.shape
    wide = ggu.shape[2]
    shape = lambda dtype, *dims: jax.ShapeDtypeStruct((packs, block) + dims, dtype)
    return pl.pallas_call(
        ordered(middle_kernel, 13, after),
        grid=(packs // STEP,),
        in_specs=[SMEM, per_pack(block, width, packs=STEP), per_pack(block, wide, packs=STEP), per_pack(block, width, packs=STEP)]
        + [fixed(1, width)]
        + [ANY] * (8 + len(after)),
        out_specs=[per_pack(block, width, packs=STEP)] * 3,
        out_shape=[
            shape(F32, width),
            shape(BF16, width),
            shape(BF16, width),
        ],
        scratch_shapes=[
            pltpu.VMEM((width, width), BF16),
            pltpu.VMEM((width, wide), BF16),
            pltpu.SemaphoreType.DMA((2, 4)),
        ],
        compiler_params=PARAMS,
        cost_estimate=cost(8, 20),
        name="middle_back",
    )(me, middle, ggu, upstream, gain, *out_shards, *in_shards, *after)


GROUP = 3 * PAIR


def attend_back_kernel(
    me_ref, q_ref, k_ref, v_ref, probs_ref, gmix_ref, cos_ref, sin_ref, dqkv_ref
):
    block = q_ref.shape[1]
    lane, first = head_lanes()
    cos, sin = cos_ref[...], -sin_ref[...]
    own = slice(HALF, HALF + block)
    dqkv_ref[0, :HALF, :GROUP] = jnp.zeros((HALF, GROUP), BF16)
    dqkv_ref[0, HALF + block :, :GROUP] = jnp.zeros((HALF, GROUP), BF16)
    for p in range(GROUP // PAIR):
        cols = slice(p * PAIR, (p + 1) * PAIR)
        dqs, dks, dvs = [], [], []
        for b in range(block // QROWS):
            rows = slice(b * QROWS, (b + 1) * QROWS)
            window = slice(b * QROWS, b * QROWS + WIN)
            q2 = stacked(q_ref[0, rows, cols], first, HEAD ** -0.5)
            do2 = stacked(gmix_ref[0, rows, cols], first, 1.0)
            probs = probs_ref[0, p, b]
            wide = probs.astype(F32)
            dprobs = dot_nt(do2, v_ref[0, window, cols])
            inner = jnp.sum(dprobs * wide, axis=-1, keepdims=True)
            ds = (wide * (dprobs - inner)).astype(BF16)
            dq2 = dot_nn(ds, k_ref[0, window, cols])
            dqs.append(jnp.where(first, dq2[:QROWS], dq2[QROWS:]) * (HEAD ** -0.5))
            dks.append(dot_tn(ds, q2))
            dvs.append(dot_tn(probs, do2))
        dq = jnp.concatenate(dqs, axis=0)
        over = WIN - QROWS
        merge = lambda a, b: jnp.concatenate([a[:QROWS], a[QROWS:] + b[:over], b[over:]], axis=0)
        dk, dv = merge(*dks), merge(*dvs)
        at = lambda n: slice(n * GROUP + p * PAIR, n * GROUP + (p + 1) * PAIR)
        dqkv_ref[0, own, at(0)] = (dq * cos[own] + turned(dq, lane) * sin[own]).astype(BF16)
        dqkv_ref[0, :, at(1)] = (dk * cos + turned(dk, lane) * sin).astype(BF16)
        dqkv_ref[0, :, at(2)] = dv.astype(BF16)


def attend_back(group, after, me, q, kv, probs, gmix, cos, sin):
    packs, block, width = q.shape
    span = block + 2 * HALF
    blocks, groups = block // QROWS, width // GROUP
    cols = lambda rows, g: pl.BlockSpec((1, rows, GROUP), lambda i: (i, 0, g))
    return pl.pallas_call(
        ordered(attend_back_kernel, 8, after),
        grid=(packs,),
        in_specs=[
            SMEM,
            cols(block, group),
            cols(span, group),
            cols(span, groups + group),
            pl.BlockSpec(
                (1, GROUP // PAIR, blocks, 2 * QROWS, WIN), lambda i: (i, group, 0, 0, 0)
            ),
            cols(block, group),
            fixed(span, PAIR),
            fixed(span, PAIR),
        ]
        + [ANY] * len(after),
        out_specs=per_pack(span, 3 * GROUP),
        out_shape=jax.ShapeDtypeStruct((packs, span, 3 * GROUP), BF16),
        compiler_params=PARAMS,
        cost_estimate=cost(8, 10),
        name="attend_back",
    )(me, q, kv, kv, probs, gmix, cos, sin, *after)


def halo_back_kernel(
    me_ref, l0, l1, r0, r1, s0, s1, s2, s3, left_ref, right_ref, w_ref, sems
):
    copies = stage_weight(me_ref[0], (s0, s1, s2, s3), w_ref, sems)
    width = left_ref.shape[2]

    @pl.when(pl.program_id(0) == 0)
    def _():
        for copy in copies:
            copy.start()
        for copy in copies:
            copy.wait()

    parts = [
        jnp.concatenate([rows_of(left)[:, GROUP:], rows_of(right)[:, GROUP:]], axis=0)
        for left, right in ((l0, r0), (l1, r1))
    ]
    rows = jnp.concatenate(
        [part[:, n * GROUP : (n + 1) * GROUP] for n in range(2) for part in parts], axis=1
    )
    grads = dot_nt(rows, w_ref[:, width:])
    half = grads.shape[0] // 2
    put(left_ref, grads[:half])
    put(right_ref, grads[half:])


def halo_back(after, me, parts, shards):
    packs, span, _ = parts[0].shape
    width = shards[0].shape[1] // 3
    edge = lambda n: pl.BlockSpec((packs, HALF, 3 * GROUP), lambda i: (i, n, 0))
    return pl.pallas_call(
        ordered(halo_back_kernel, 9, after),
        grid=(1,),
        in_specs=[SMEM] + [edge(0)] * 2 + [edge(span // HALF - 1)] * 2
        + [ANY] * (4 + len(after)),
        out_specs=[per_pack(HALF, width, packs=packs)] * 2,
        out_shape=[jax.ShapeDtypeStruct((packs, HALF, width), BF16)] * 2,
        scratch_shapes=[pltpu.VMEM((width, 3 * width), BF16), pltpu.SemaphoreType.DMA((4,))],
        compiler_params=PARAMS,
        cost_estimate=cost(1.2, 6),
        name="halo_back",
    )(me, *parts, *parts, *shards, *after)


def own_back_kernel(me_ref, p0, p1, s0, s1, s2, s3, own_ref, w_ref, sems):
    copies = stage_weight(me_ref[0], (s0, s1, s2, s3), w_ref, sems)
    block = own_ref.shape[1]

    @pl.when(pl.program_id(0) == 0)
    def _():
        for copy in copies:
            copy.start()
        for copy in copies:
            copy.wait()

    own = slice(HALF, HALF + block)
    parts = [part[:, own, :].reshape(-1, part.shape[2]) for part in (p0, p1)]
    rows = jnp.concatenate(
        [part[:, n * GROUP : (n + 1) * GROUP] for n in range(3) for part in parts], axis=1
    )
    put(own_ref, dot_nt(rows, w_ref[...]))


def own_back(after, me, parts, shards):
    packs, span, _ = parts[0].shape
    block, width = span - 2 * HALF, shards[0].shape[1] // 3
    return pl.pallas_call(
        ordered(own_back_kernel, 7, after),
        grid=(packs // STEP,),
        in_specs=[SMEM] + [per_pack(span, 3 * GROUP, packs=STEP)] * 2
        + [ANY] * (4 + len(after)),
        out_specs=per_pack(block, width, packs=STEP),
        out_shape=jax.ShapeDtypeStruct((packs, block, width), F32),
        scratch_shapes=[pltpu.VMEM((width, 3 * width), BF16), pltpu.SemaphoreType.DMA((4,))],
        compiler_params=PARAMS,
        cost_estimate=cost(5, 15),
        name="own_back",
    )(me, *parts, *shards, *after)


def finish_kernel(x_ref, own_ref, fl_ref, fr_ref, gm_ref, gain_ref, out_ref):
    block = x_ref.shape[1]
    normal, inverse = norm_of(x_ref[0].astype(F32))
    grad = own_ref[0]
    grad = jnp.concatenate(
        [
            grad[:HALF] + fl_ref[0].astype(F32),
            grad[HALF : block - HALF],
            grad[block - HALF :] + fr_ref[0].astype(F32),
        ],
        axis=0,
    )
    out_ref[0] = (gm_ref[0] + norm_back(grad, normal, inverse, gain_ref[...])).astype(BF16)


def finish(after, tokens, own, from_left, from_right, grad_middle, gain):
    packs, block, width = tokens.shape
    per_pack = lambda *dims: pl.BlockSpec((1,) + dims, lambda i: (i,) + (0,) * len(dims))
    return pl.pallas_call(
        ordered(finish_kernel, 6, after),
        grid=(packs,),
        in_specs=[
            per_pack(block, width),
            per_pack(block, width),
            per_pack(HALF, width),
            per_pack(HALF, width),
            per_pack(block, width),
            pl.BlockSpec((1, width), lambda i: (0, 0)),
        ]
        + [ANY] * len(after),
        out_specs=per_pack(block, width),
        out_shape=jax.ShapeDtypeStruct((packs, block, width), BF16),
        cost_estimate=pl.CostEstimate(flops=20_000_000, bytes_accessed=10_000_000, transcendentals=0),
        name="finish",
    )(tokens, own, from_left, from_right, grad_middle, gain, *after)


def tables(start, count):
    half_size = HEAD // 2
    freqs = jnp.power(THETA, -jnp.arange(half_size, dtype=F32) * (2.0 / HEAD))
    positions = (start + jnp.arange(count, dtype=jnp.int32)).astype(F32)
    angles = positions[:, None] * freqs[None, :]
    cos, sin = jnp.cos(angles), jnp.sin(angles)
    return (
        jnp.concatenate([cos, cos, cos, cos], axis=-1),
        jnp.concatenate([-sin, sin, -sin, sin], axis=-1),
    )


def weight_grad(left, right):
    return dot_tn(
        left.reshape(-1, left.shape[-1]), right.reshape(-1, right.shape[-1])
    ).astype(BF16)


def gain_grad(grad, weight, gain):
    return jnp.sum(grad * weight.astype(F32), axis=1) / gain.astype(F32)


def per_device(tokens, doc_begin, gain_attn, w_qkv, w_att_out, gain_mlp, w_in, w_down, cotangent):
    packs, block, width = tokens.shape
    me_w, me_c = lax.axis_index("wsh"), lax.axis_index("ctx")
    me = me_w.reshape(1).astype(jnp.int32)
    part = gain_attn.shape[0]

    row = jnp.zeros((16, w_qkv.shape[1]), BF16)
    row = lax.dynamic_update_slice(row, gain_attn[None], (0, me_w * part))
    row = lax.dynamic_update_slice(row, gain_mlp[None], (0, width + me_w * part))
    qkv = jnp.concatenate([w_qkv, row], axis=0)
    qkv_near, qkv_far = swap(qkv, "wsh", 1), swap(qkv, "wsh", 2)
    halo_left = shifted(tokens[:, block - HALF :], "ctx", 1)
    doc_rows = jnp.broadcast_to(doc_begin.astype(BF16)[:, :, None], (packs, 16, width))
    halo_right = shifted(jnp.concatenate([tokens[:, :HALF], doc_rows], axis=1), "ctx", -1)
    both = jnp.concatenate([w_att_out, w_down], axis=0)
    at_x, half_rows = me_c % 2, part // 2
    in_half = lax.dynamic_slice_in_dim(w_in, at_x * half_rows, half_rows, 0)
    qkv_far, halo_left, halo_right, in_half, both = lax.optimization_barrier(
        (qkv_far, halo_left, halo_right, in_half, both)
    )
    in_half = swap(in_half, "wsh", 2)
    both_far = swap(both, "wsh", 2)
    qkv_shards = (qkv, qkv_near, qkv_far, swap(qkv_far, "wsh", 1))
    gain_rows = sum(shard[part : part + 1].astype(F32) for shard in qkv_shards)
    gain_one, gain_two = gain_rows[:, :width], gain_rows[:, width : 2 * width]
    doc_right = halo_right[:, HALF, 0].astype(jnp.int32)
    left_ok = (doc_begin[:, 0] < me_c).astype(jnp.int32)
    right_ok = (
        (doc_right == doc_begin[:, 0]) & (me_c + 1 < lax.axis_size("ctx"))
    ).astype(jnp.int32)
    cos, sin = tables(me_c * block - HALF, block + 2 * HALF)


    q, kv, first_in = project(
        me, tokens, halo_left, halo_right, cos, sin, qkv_shards
    )
    in_half, q = lax.optimization_barrier((in_half, q))
    in_other = swap(in_half, "ctx", 1)
    both_near, in_near = swap(both, "wsh", 1), swap(w_in, "wsh", 1)
    probs, mixed = attend((), left_ok, right_ok, q, kv)
    both_far, in_half, in_other, both_near, in_near, mixed = lax.optimization_barrier(
        (both_far, in_half, in_other, both_near, in_near, mixed)
    )
    both_far_near = swap(both_far, "wsh", 1)
    in_far = joined(in_half, in_other, at_x, 0)
    in_far_near = swap(in_far, "wsh", 1)
    in_shards = (w_in, in_near, in_far, in_far_near)
    both_shards = (both, both_near, both_far, both_far_near)

    output, second_in, hidden, ggu, middle = hidden_layer(
        me, tokens, mixed, cotangent, gain_two, both_shards, in_shards
    )
    grad = weight_grad(second_in, ggu)
    sum_in = Reduction(grad, bits=(2, 1))
    sum_in.value, hidden = lax.optimization_barrier((sum_in.value, hidden))
    sum_in.begin_core()
    sum_both = Reduction(weight_grad(hidden, cotangent), bits=(2, 1))
    (sum_both.value,) = meet((sum_in,), sum_both.value)
    sum_in.end_core()
    sum_in.begin_side()
    sum_both.begin_core()
    grad_middle, low, gmix = middle_back(
        (sum_in.value, sum_both.value),
        me, middle, ggu, cotangent, gain_two, both_shards, in_shards,
    )
    low, gmix = meet((sum_both, sum_in), low, gmix)
    sum_both.end_core()
    sum_in.end_side()
    depart(sum_in, sum_both)
    sum_in.begin_across()
    sum_out = Reduction(weight_grad(mixed, low))
    sum_out.begin_core()
    sum_out.end_core()
    sum_both.join(sum_out)
    sum_both.begin_side()
    back = lambda group, *after: attend_back(group, after, me, q, kv, probs, gmix, cos, sin)
    back_0 = back(0, sum_in.value, sum_both.value)
    (back_0,) = meet((sum_in, sum_both), back_0)
    sum_in.end_across()
    sum_both.end_side()
    sum_in.value, sum_both.value, back_0 = lax.optimization_barrier(
        (sum_in.value, sum_both.value, back_0)
    )
    sum_in.begin_near()
    sum_both.begin_across()
    grad_0 = weight_grad(first_in, back_0)
    (grad_0,) = meet((sum_in,), grad_0)
    sum_0 = Reduction(grad_0)
    sum_in.end_near()
    sum_in.begin_far()
    sum_0.begin_core()
    sum_0.end_core()
    sum_0.begin_side()
    back_1 = back(1, sum_in.value, sum_0.value, sum_both.value)
    (back_1,) = meet((sum_in, sum_both), back_1)
    sum_in.end_far()
    sum_both.end_across()
    sum_in.value, sum_both.value, back_1 = lax.optimization_barrier(
        (sum_in.value, sum_both.value, back_1)
    )
    sum_in.begin_spread()
    sum_both.begin_near()
    grad_1 = weight_grad(first_in, back_1)
    (grad_1,) = meet((sum_in, sum_0, sum_both), grad_1)
    sum_1 = Reduction(grad_1)
    sum_in.end_spread()
    sum_0.end_side()
    sum_both.end_near()
    depart(sum_in, sum_0, sum_both)
    sum_in.begin_last()
    sum_0.begin_across()
    sum_both.begin_far()
    sum_1.begin_core()
    sum_1.end_core()
    sum_1.begin_side()
    parts = (back_0, back_1)
    to_left, to_right = halo_back(
        (sum_1.value, sum_in.value, sum_0.value, sum_both.value), me, parts, qkv_shards
    )
    to_left, to_right = meet((sum_0,), to_left, to_right)
    sum_0.end_across()
    sum_0.begin_near()
    own = own_back((sum_0.value,), me, parts, qkv_shards)
    to_left, to_right, own = meet((sum_0, sum_both, sum_1, sum_in), to_left, to_right, own)
    sum_1.end_side()
    sum_0.end_near()
    sum_both.end_far()
    depart(sum_0, sum_1, sum_both)
    sum_1.begin_across()
    sum_0.begin_far()
    sum_both.begin_spread()
    to_left, to_right = meet((sum_0, sum_1), to_left, to_right)
    sum_1.end_across()
    sum_0.end_far()
    depart(sum_0, sum_1)
    sum_1.begin_near()
    from_right = shifted(to_left, "ctx", -1)
    from_left = shifted(to_right, "ctx", 1)
    sum_0.begin_spread()
    meet((sum_0, sum_1, sum_both))
    sum_1.end_near()
    sum_0.end_spread()
    sum_both.end_spread()
    depart(sum_0, sum_1, sum_both)
    sum_1.begin_far()
    sum_both.begin_last()
    meet((sum_1,))
    sum_1.end_far()
    sum_1.begin_spread()
    from_left, from_right = meet((sum_1,), from_left, from_right)
    sum_1.end_spread()
    depart(sum_0, sum_1)
    sum_1.begin_last()
    sum_0.begin_last()
    grad_tokens = finish(
        (sum_1.value,), tokens, own, from_left, from_right, grad_middle, gain_one
    )
    (grad_tokens,) = meet((sum_0, sum_1, sum_both), grad_tokens)
    grad_in = sum_in.end_last()
    grad_both = sum_both.end_last()
    pieces = [sum_0.end_last(), sum_1.end_last()]
    grad_qkv = jnp.concatenate(
        [item[:, n * GROUP : (n + 1) * GROUP] for n in range(3) for item in pieces], axis=1
    )
    down = w_down.shape[0]
    return (
        output, grad_tokens, gain_grad(grad_qkv, w_qkv, gain_attn), grad_qkv, grad_both[down:],
        gain_grad(grad_in, w_in, gain_mlp), grad_in, grad_both[:down],
    )


def solution(mesh):
    return jax.shard_map(
        per_device,
        mesh=mesh,
        in_specs=(
            P("wsh", "ctx", None),
            P("wsh", "ctx"),
            P("wsh"),
            P("wsh", None),
            P("wsh", None),
            P("wsh"),
            P("wsh", None),
            P("wsh", None),
            P("wsh", "ctx", None),
        ),
        out_specs=(
            P("wsh", "ctx", None),
            P("wsh", "ctx", None),
            P("wsh"),
            P("wsh", None),
            P("wsh", None),
            P("wsh"),
            P("wsh", None),
            P("wsh", None),
        ),
        check_vma=False,
    )
```

```python
import functools
import math

import jax
import jax.numpy as jnp
from jax import lax
from jax.experimental import pallas as pl
from jax.experimental.pallas import tpu as pltpu
from jax.sharding import PartitionSpec as P

HEAD = 64
HALF = 64
EPS = 1e-05
THETA = 10000.0
MASKED = -1e30
PAIR = 2 * HEAD
QROWS = 128
WIN = QROWS + 2 * HALF
VMEM_BYTES = 56 * 1024 * 1024
STEP = 1

F32 = jnp.float32
BF16 = jnp.bfloat16


def dot_nn(left, right):
    return jnp.dot(left, right, preferred_element_type=F32)


def dot_nt(left, right):
    return lax.dot_general(left, right, (((1,), (1,)), ((), ())), preferred_element_type=F32)


def dot_tn(left, right):
    return lax.dot_general(left, right, (((0,), (0,)), ((), ())), preferred_element_type=F32)


def swap(value, axis, bit):
    peers = lax.axis_size(axis)
    return lax.ppermute(value, axis, [(i, i ^ bit) for i in range(peers)])


def shifted(value, axis, by):
    peers = lax.axis_size(axis)
    return lax.ppermute(value, axis, [(i, i + by) for i in range(peers) if 0 <= i + by < peers])


def pick(value, index, axis=0):
    return lax.dynamic_index_in_dim(value, index, axis, keepdims=False)


def added(kept, *received):
    total = kept.astype(F32)
    for item in received:
        total = total + item.astype(F32)
    return total.astype(BF16)


class Reduction:
    def __init__(self, grad, bits=(1, 2)):
        self.bits = bits
        self.me_w, self.me_c = lax.axis_index("wsh"), lax.axis_index("ctx")
        self.at_first, self.at_second = (self.me_c // bit % 2 for bit in bits)
        self.value = grad.reshape(2, 2, grad.shape[0] // 4, grad.shape[1])
        self.small = lax.axis_size("ctx") == 8
        self.got = ()

    def begin(self, send, axis, bit):
        self.got = (swap(send, axis, bit),)

    def begin_core(self):
        self.got = (swap(pick(self.value, 1 - self.me_w % 2, 1), "wsh", 1),)

    def end_core(self):
        self.value = added(pick(self.value, self.me_w % 2, 1), *self.got)
        return self.value

    def join(self, other):
        self.value = jnp.concatenate([self.value, other.value], axis=1)

    def begin_side(self):
        self.begin(pick(self.value, 1 - self.me_w // 2), "wsh", 2)

    def end_side(self):
        self.value = added(pick(self.value, self.me_w // 2), *self.got)
        self.half, self.chunk = self.value.shape[1] // 2, self.value.shape[0] // 2
        return self.value

    def halves(self, index):
        return lax.dynamic_slice_in_dim(self.value, index * self.half, self.half, 1)

    def chunks(self, index):
        return lax.dynamic_slice_in_dim(self.value, index * self.chunk, self.chunk, 0)

    def begin_across(self):
        self.got = ()
        if self.small:
            self.begin(self.halves(1 - self.at_first), "ctx", self.bits[0])

    def end_across(self):
        if self.small:
            self.value = added(self.halves(self.at_first), *self.got)
        return self.value

    def begin_near(self):
        self.got = ()
        if self.small:
            self.begin(self.chunks(1 - self.at_second), "ctx", self.bits[1])

    def end_near(self):
        if self.small:
            self.value = added(self.chunks(self.at_second), *self.got)
        return self.value

    def quarters(self, first, second):
        return lax.dynamic_slice(
            self.value, (second * self.chunk, first * self.half), (self.chunk, self.half)
        )

    def begin_plane(self):
        self.got = ()
        if self.small:
            first, second = self.bits
            self.got = tuple(
                swap(self.quarters(self.at_first ^ f, self.at_second ^ s), "ctx", f * first + s * second)
                for f, s in ((1, 1), (0, 1), (1, 0))
            )

    def end_plane(self):
        if self.small:
            self.value = added(self.quarters(self.at_first, self.at_second), *self.got)
        return self.value

    def begin_gather(self):
        self.got = ()
        if self.small:
            first, second = self.bits
            self.got = tuple(
                swap(self.value, "ctx", f * first + s * second) for f, s in ((1, 1), (0, 1), (1, 0))
            )

    def end_gather(self):
        if not self.small:
            return lax.psum(self.value.astype(F32), "ctx")
        across, second, first = self.got
        return joined(
            joined(self.value, second, self.at_second, 0),
            joined(first, across, self.at_second, 0),
            self.at_first,
            1,
        ).astype(F32)

    def begin_far(self):
        self.got = ()
        if self.small:
            self.begin(self.value, "ctx", 4)

    def end_far(self):
        if self.small:
            self.value = added(self.value, *self.got)
        return self.value

    def begin_spread(self):
        self.got = ()
        if self.small:
            self.begin(self.value, "ctx", self.bits[1])

    def end_spread(self):
        if self.small:
            self.value = joined(self.value, *self.got, self.at_second, 0)
        return self.value

    def begin_last(self):
        self.got = ()
        if self.small:
            self.begin(self.value, "ctx", self.bits[0])

    def end_last(self):
        if not self.small:
            return lax.psum(self.value.astype(F32), "ctx")
        return joined(self.value, *self.got, self.at_first, 1).astype(F32)


def meet(sums, *arrays):
    out = list(
        lax.optimization_barrier(sum((item.got for item in sums), ()) + arrays)
    )
    for item in sums:
        item.got, out = tuple(out[: len(item.got)]), out[len(item.got) :]
    return out


def depart(*sums):
    for item, value in zip(sums, lax.optimization_barrier(tuple(item.value for item in sums))):
        item.value = value


def joined(mine, other, place, axis):
    low = jnp.where(place == 0, mine, other)
    high = jnp.where(place == 0, other, mine)
    return jnp.concatenate([low, high], axis=axis)


def stage_weight(me, shards, scratch, sems, start=0):
    rows = scratch.shape[0] // 4
    return [
        pltpu.make_async_copy(
            shard.at[pl.ds(start, rows)], scratch.at[pl.ds(pl.multiple_of((me ^ k) * rows, rows), rows)], sems.at[k]
        )
        for k, shard in enumerate(shards)
    ]


def norm_of(values):
    average = jnp.mean(values, axis=-1, keepdims=True)
    centred = values - average
    inverse = lax.rsqrt(jnp.mean(centred * centred, axis=-1, keepdims=True) + EPS)
    return centred * inverse, inverse


def norm_back(incoming, normal, inverse, gain):
    scaled = incoming * gain
    return inverse * (
        scaled
        - jnp.mean(scaled, axis=-1, keepdims=True)
        - normal * jnp.mean(scaled * normal, axis=-1, keepdims=True)
    )


def head_lanes():
    lane = lax.broadcasted_iota(jnp.int32, (1, PAIR), 1)
    return lane, lane < HEAD


def turned(value, lane):
    ahead = pltpu.roll(value, PAIR - HEAD // 2, 1)
    behind = pltpu.roll(value, HEAD // 2, 1)
    return jnp.where(lane % HEAD < HEAD // 2, ahead, behind)


def stacked(value, first, scale):
    one = jnp.where(first, scale, 0.0).astype(BF16)
    two = jnp.where(first, 0.0, scale).astype(BF16)
    return jnp.concatenate([value * one, value * two], axis=0)


def per_pack(*dims, packs=1):
    return pl.BlockSpec((packs,) + dims, lambda i: (i,) + (0,) * len(dims))


def rows_of(ref):
    return ref[...].reshape(-1, ref.shape[-1])


def put(ref, value):
    ref[...] = value.astype(ref.dtype).reshape(ref.shape)


def fixed(*dims):
    return pl.BlockSpec(dims, lambda i: (0,) * len(dims))


def cost(gflops, megabytes):
    return pl.CostEstimate(
        flops=int(gflops * 1e8), bytes_accessed=int(megabytes * 1e5), transcendentals=0
    )


def ordered(kernel, count, after):
    return lambda *refs: kernel(*refs[:count], *refs[count + len(after) :])


SMEM = pl.BlockSpec(memory_space=pltpu.SMEM)
ANY = pl.BlockSpec(memory_space=pl.ANY)
PARAMS = pltpu.CompilerParams(vmem_limit_bytes=VMEM_BYTES)


def project_kernel(
    me_ref, x_ref, hl_ref, hr_ref, cos_ref, sin_ref, s0, s1, s2, s3,
    q_ref, kv_ref, first_ref, w_ref, gain_ref, sems, gain_sems,
):
    pack = pl.program_id(0)
    block = x_ref.shape[1]
    width = x_ref.shape[2]
    shards = (s0, s1, s2, s3)
    copies = stage_weight(me_ref[0], shards, w_ref, sems)
    gains = [
        pltpu.make_async_copy(
            shard.at[pl.ds(width // 4, 16), pl.ds(0, width)], gain_ref.at[n], gain_sems.at[n]
        )
        for n, shard in enumerate(shards)
    ]

    @pl.when(pack == 0)
    def _():
        for copy in gains + copies:
            copy.start()
        for copy in gains:
            copy.wait()

    values = jnp.concatenate([hl_ref[0], x_ref[0], hr_ref[0]], axis=0).astype(F32)
    normal, _ = norm_of(values)
    gain = jnp.sum(gain_ref[...].astype(F32), axis=0)[:1]
    first_ref[0] = (normal * gain).astype(BF16)
    lane, first = head_lanes()
    cos, sin = cos_ref[...], sin_ref[...]
    own = slice(HALF, HALF + block)
    step = 2 * PAIR

    @pl.when(pack == 0)
    def _():
        for copy in copies:
            copy.wait()

    for j in range(width // step):
        cols = slice(j * step, (j + 1) * step)
        q = dot_nn(first_ref[0, own, :], w_ref[:, cols])
        k = dot_nn(first_ref[0], w_ref[:, width + j * step : width + (j + 1) * step])
        v = dot_nn(first_ref[0], w_ref[:, 2 * width + j * step : 2 * width + (j + 1) * step])
        for i in range(2):
            part = slice(i * PAIR, (i + 1) * PAIR)
            base = j * step + i * PAIR
            qp, kp = q[:, part], k[:, part]
            q_ref[0, :, base : base + PAIR] = (
                qp * cos[own] + turned(qp, lane) * sin[own]
            ).astype(BF16)
            kv_ref[0, :, base : base + PAIR] = (kp * cos + turned(kp, lane) * sin).astype(BF16)
        kv_ref[0, :, width + j * step : width + (j + 1) * step] = v.astype(BF16)


def project(me, tokens, halo_left, halo_right, cos, sin, shards):
    packs, block, width = tokens.shape
    span = block + 2 * HALF
    return pl.pallas_call(
        project_kernel,
        grid=(packs,),
        in_specs=[SMEM, per_pack(block, width), per_pack(HALF, width), per_pack(HALF, width)]
        + [fixed(span, PAIR), fixed(span, PAIR)]
        + [ANY] * 4,
        out_specs=[per_pack(block, width), per_pack(span, 2 * width), per_pack(span, width)],
        out_shape=[
            jax.ShapeDtypeStruct((packs, block, width), BF16),
            jax.ShapeDtypeStruct((packs, span, 2 * width), BF16),
            jax.ShapeDtypeStruct((packs, span, width), BF16),
        ],
        scratch_shapes=[
            pltpu.VMEM((width, 3 * width), BF16),
            pltpu.VMEM((4, 16, width), BF16),
            pltpu.SemaphoreType.DMA((4,)),
            pltpu.SemaphoreType.DMA((4,)),
        ],
        compiler_params=PARAMS,
        cost_estimate=cost(5, 15),
        name="project",
    )(me, tokens, halo_left, halo_right, cos, sin, *shards)


def attend_kernel(left_ok, right_ok, q_ref, kv_ref, probs_ref, mixed_ref):
    pack = pl.program_id(0)
    block, width = q_ref.shape[1], q_ref.shape[2]
    _, first = head_lanes()
    row = lax.broadcasted_iota(jnp.int32, (QROWS, WIN), 0)
    col = lax.broadcasted_iota(jnp.int32, (QROWS, WIN), 1)
    near = (col >= row) & (col <= row + 2 * HALF)
    blocks = block // QROWS
    for b in range(blocks):
        allowed = near
        if b == 0:
            allowed = allowed & ((col >= HALF) | (left_ok[pack] > 0))
        if b == blocks - 1:
            allowed = allowed & ((col < WIN - HALF) | (right_ok[pack] > 0))
        bias = jnp.where(allowed, 0.0, MASKED)
        bias = jnp.concatenate([bias, bias], axis=0)
        rows = slice(b * QROWS, (b + 1) * QROWS)
        window = slice(b * QROWS, b * QROWS + WIN)
        for p in range(width // PAIR):
            cols = slice(p * PAIR, (p + 1) * PAIR)
            q2 = stacked(q_ref[0, rows, cols], first, HEAD ** -0.5)
            scores = dot_nt(q2, kv_ref[0, window, cols]) + bias
            powers = jnp.exp(scores - jnp.max(scores, axis=-1, keepdims=True))
            probs = (powers * (1.0 / jnp.sum(powers, axis=-1, keepdims=True))).astype(BF16)
            probs_ref[0, p, b] = probs
            out = dot_nn(probs, kv_ref[0, window, width + p * PAIR : width + (p + 1) * PAIR])
            mixed_ref[0, rows, cols] = jnp.where(first, out[:QROWS], out[QROWS:]).astype(BF16)


def attend(after, left_ok, right_ok, q, kv):
    packs, block, width = q.shape
    pairs, blocks = width // PAIR, block // QROWS
    return pl.pallas_call(
        ordered(attend_kernel, 4, after),
        grid=(packs,),
        in_specs=[SMEM, SMEM, per_pack(block, width), per_pack(block + 2 * HALF, 2 * width)]
        + [ANY] * len(after),
        out_specs=[per_pack(pairs, blocks, 2 * QROWS, WIN), per_pack(block, width)],
        out_shape=[
            jax.ShapeDtypeStruct((packs, pairs, blocks, 2 * QROWS, WIN), BF16),
            jax.ShapeDtypeStruct((packs, block, width), BF16),
        ],
        compiler_params=PARAMS,
        cost_estimate=cost(10, 15),
        name="attend",
    )(left_ok, right_ok, q, kv, *after)


def hidden_kernel(
    me_ref, x_ref, mixed_ref, up_ref, gain_ref, o0, o1, o2, o3, i0, i1, i2, i3,
    out_ref, second_ref, hidden_ref, ggu_ref, middle_ref,
    wo_ref, wi_ref, wd_ref, sems,
):
    tile = pl.program_id(0)
    ff = wd_ref.shape[0]
    both = (o0, o1, o2, o3)
    copies = [
        stage_weight(me_ref[0], both, wo_ref, sems.at[0]),
        stage_weight(me_ref[0], (i0, i1, i2, i3), wi_ref, sems.at[1]),
        stage_weight(me_ref[0], both, wd_ref, sems.at[2], wo_ref.shape[0] // 4),
    ]

    @pl.when(tile == 0)
    def _():
        for group in copies:
            for copy in group:
                copy.start()
        for copy in copies[0]:
            copy.wait()

    middle = rows_of(x_ref).astype(F32) + dot_nn(rows_of(mixed_ref), wo_ref[...])
    put(middle_ref, middle)
    normal, _ = norm_of(middle)
    second = (normal * gain_ref[...]).astype(BF16)
    put(second_ref, second)
    upstream = rows_of(up_ref)

    @pl.when(tile == 0)
    def _():
        for group in copies[1:]:
            for copy in group:
                copy.wait()

    step = 384
    result = middle
    for j in range(ff // step):
        cols = slice(j * step, (j + 1) * step)
        ups = slice(ff + j * step, ff + (j + 1) * step)
        gate = dot_nn(second, wi_ref[:, cols])
        up = dot_nn(second, wi_ref[:, ups])
        grad_hidden = dot_nt(upstream, wd_ref[cols, :])
        cumulative = 0.5 + 0.5 * lax.erf(gate * (0.5 ** 0.5))
        activated = gate * cumulative
        density = jnp.exp(-0.5 * gate * gate) * (1.0 / math.sqrt(2.0 * math.pi))
        hidden = (activated * up).astype(BF16)
        put(hidden_ref.at[:, :, cols], hidden)
        put(ggu_ref.at[:, :, cols], grad_hidden * up * (cumulative + gate * density))
        put(ggu_ref.at[:, :, ups], grad_hidden * activated)
        result = result + dot_nn(hidden, wd_ref[cols, :])
    put(out_ref, result)


def hidden_layer(me, tokens, mixed, upstream, gain, both_shards, in_shards):
    packs, block, width = tokens.shape
    ff = in_shards[0].shape[1] // 2
    shape = lambda dtype, *dims: jax.ShapeDtypeStruct((packs, block) + dims, dtype)
    return pl.pallas_call(
        hidden_kernel,
        grid=(packs // STEP,),
        in_specs=[SMEM] + [per_pack(block, width, packs=STEP)] * 3 + [fixed(1, width)] + [ANY] * 8,
        out_specs=[
            per_pack(block, width, packs=STEP),
            per_pack(block, width, packs=STEP),
            per_pack(block, ff, packs=STEP),
            per_pack(block, 2 * ff, packs=STEP),
            per_pack(block, width, packs=STEP),
        ],
        out_shape=[
            shape(BF16, width),
            shape(BF16, width),
            shape(BF16, ff),
            shape(BF16, 2 * ff),
            shape(BF16, width),
        ],
        scratch_shapes=[
            pltpu.VMEM((width, width), BF16),
            pltpu.VMEM((width, 2 * ff), BF16),
            pltpu.VMEM((ff, width), BF16),
            pltpu.SemaphoreType.DMA((3, 4)),
        ],
        compiler_params=PARAMS,
        cost_estimate=cost(16, 25),
        name="hidden_layer",
    )(me, tokens, mixed, upstream, gain, *both_shards, *in_shards)


def middle_kernel(
    me_ref, middle_ref, ggu_ref, up_ref, mixed_ref, gain_ref, o0, o1, o2, o3, i0, i1, i2, i3,
    low_ref, gmix_ref, gout_ref, wo_ref, wi_ref, total_ref, sems,
):
    tile = pl.program_id(0)
    copies = [
        stage_weight(me_ref[0], group, scratch, sems.at[n])
        for n, (group, scratch) in enumerate(
            (((o0, o1, o2, o3), wo_ref), ((i0, i1, i2, i3), wi_ref))
        )
    ]

    @pl.when(tile == 0)
    def _():
        for group in copies:
            for copy in group:
                copy.start()
        total_ref[...] = jnp.zeros_like(total_ref)

    normal, inverse = norm_of(rows_of(middle_ref).astype(F32))

    @pl.when(tile == 0)
    def _():
        for group in copies:
            for copy in group:
                copy.wait()

    grad_second = dot_nt(rows_of(ggu_ref), wi_ref[...])
    grad_middle = rows_of(up_ref).astype(F32) + norm_back(grad_second, normal, inverse, gain_ref[...])
    low = grad_middle.astype(BF16)
    put(low_ref, low)
    put(gmix_ref, dot_nt(low, wo_ref[...]))
    total_ref[...] += dot_tn(rows_of(mixed_ref), low)

    @pl.when(tile == pl.num_programs(0) - 1)
    def _():
        gout_ref[...] = total_ref[...].astype(BF16)


def middle_back(after, me, middle, ggu, upstream, mixed, gain, out_shards, in_shards):
    packs, block, width = middle.shape
    wide = ggu.shape[2]
    shape = lambda dtype, *dims: jax.ShapeDtypeStruct((packs, block) + dims, dtype)
    return pl.pallas_call(
        ordered(middle_kernel, 14, after),
        grid=(packs // STEP,),
        in_specs=[SMEM, per_pack(block, width, packs=STEP), per_pack(block, wide, packs=STEP)]
        + [per_pack(block, width, packs=STEP)] * 2
        + [fixed(1, width)]
        + [ANY] * (8 + len(after)),
        out_specs=[per_pack(block, width, packs=STEP)] * 2 + [fixed(width, width)],
        out_shape=[
            shape(BF16, width),
            shape(BF16, width),
            jax.ShapeDtypeStruct((width, width), BF16),
        ],
        scratch_shapes=[
            pltpu.VMEM((width, width), BF16),
            pltpu.VMEM((width, wide), BF16),
            pltpu.VMEM((width, width), F32),
            pltpu.SemaphoreType.DMA((2, 4)),
        ],
        compiler_params=PARAMS,
        cost_estimate=cost(8, 20),
        name="middle_back",
    )(me, middle, ggu, upstream, mixed, gain, *out_shards, *in_shards, *after)


GROUP = 3 * PAIR


def attend_back_kernel(
    me_ref, q_ref, k_ref, v_ref, probs_ref, gmix_ref, cos_ref, sin_ref, first_ref,
    dqkv_ref, grad_ref, all_ref,
):
    block = q_ref.shape[1]
    lane, first = head_lanes()
    cos, sin = cos_ref[...], -sin_ref[...]
    own = slice(HALF, HALF + block)
    dqkv_ref[0, :HALF, :GROUP] = jnp.zeros((HALF, GROUP), BF16)
    dqkv_ref[0, HALF + block :, :GROUP] = jnp.zeros((HALF, GROUP), BF16)
    for p in range(GROUP // PAIR):
        cols = slice(p * PAIR, (p + 1) * PAIR)
        blocks = range(block // QROWS)
        rows = [slice(b * QROWS, (b + 1) * QROWS) for b in blocks]
        window = [slice(b * QROWS, b * QROWS + WIN) for b in blocks]
        do2 = [stacked(gmix_ref[0, rows[b], cols], first, 1.0) for b in blocks]
        q2 = [stacked(q_ref[0, rows[b], cols], first, HEAD ** -0.5) for b in blocks]
        dprobs = [dot_nt(do2[b], v_ref[0, window[b], cols]) for b in blocks]
        dvs = [dot_tn(probs_ref[0, p, b], do2[b]) for b in blocks]
        wide = [probs_ref[0, p, b].astype(F32) for b in blocks]
        inner = [jnp.sum(dprobs[b] * wide[b], axis=-1, keepdims=True) for b in blocks]
        ds = [(wide[b] * (dprobs[b] - inner[b])).astype(BF16) for b in blocks]
        dq2 = [dot_nn(ds[b], k_ref[0, window[b], cols]) for b in blocks]
        dqs = [jnp.where(first, d[:QROWS], d[QROWS:]) * (HEAD ** -0.5) for d in dq2]
        dks = [dot_tn(ds[b], q2[b]) for b in blocks]
        dq = jnp.concatenate(dqs, axis=0)
        over = WIN - QROWS
        merge = lambda a, b: jnp.concatenate([a[:QROWS], a[QROWS:] + b[:over], b[over:]], axis=0)
        dk, dv = merge(*dks), merge(*dvs)
        at = lambda n: slice(n * GROUP + p * PAIR, n * GROUP + (p + 1) * PAIR)
        dqkv_ref[0, own, at(0)] = (dq * cos[own] + turned(dq, lane) * sin[own]).astype(BF16)
        dqkv_ref[0, :, at(1)] = (dk * cos + turned(dk, lane) * sin).astype(BF16)
        dqkv_ref[0, :, at(2)] = dv.astype(BF16)

    all_ref[pl.program_id(0)] = dqkv_ref[0]

    @pl.when(pl.program_id(0) == pl.num_programs(0) - 1)
    def _():
        for n in range(3):
            part = slice(n * GROUP, (n + 1) * GROUP)
            right = all_ref[:, :, part].reshape(-1, GROUP)
            grad_ref[:, part] = dot_tn(rows_of(first_ref), right).astype(BF16)


def attend_back(group, after, me, q, kv, probs, gmix, cos, sin, first_in):
    packs, block, width = q.shape
    span = block + 2 * HALF
    blocks, groups = block // QROWS, width // GROUP
    cols = lambda rows, g: pl.BlockSpec((1, rows, GROUP), lambda i: (i, 0, g))
    return pl.pallas_call(
        ordered(attend_back_kernel, 9, after),
        grid=(packs,),
        in_specs=[
            SMEM,
            cols(block, group),
            cols(span, group),
            cols(span, groups + group),
            pl.BlockSpec(
                (1, GROUP // PAIR, blocks, 2 * QROWS, WIN), lambda i: (i, group, 0, 0, 0)
            ),
            cols(block, group),
            fixed(span, PAIR),
            fixed(span, PAIR),
            fixed(packs, span, width),
        ]
        + [ANY] * len(after),
        out_specs=[per_pack(span, 3 * GROUP), fixed(width, 3 * GROUP)],
        out_shape=[
            jax.ShapeDtypeStruct((packs, span, 3 * GROUP), BF16),
            jax.ShapeDtypeStruct((width, 3 * GROUP), BF16),
        ],
        scratch_shapes=[pltpu.VMEM((packs, span, 3 * GROUP), BF16)],
        compiler_params=PARAMS,
        cost_estimate=cost(8, 10),
        name="attend_back",
    )(me, q, kv, kv, probs, gmix, cos, sin, first_in, *after)


def halo_back_kernel(
    me_ref, l0, l1, r0, r1, s0, s1, s2, s3, left_ref, right_ref, w_ref, sems
):
    copies = stage_weight(me_ref[0], (s0, s1, s2, s3), w_ref, sems)
    width = left_ref.shape[2]

    @pl.when(pl.program_id(0) == 0)
    def _():
        for copy in copies:
            copy.start()
        for copy in copies:
            copy.wait()

    parts = [
        jnp.concatenate([rows_of(left)[:, GROUP:], rows_of(right)[:, GROUP:]], axis=0)
        for left, right in ((l0, r0), (l1, r1))
    ]
    rows = jnp.concatenate(
        [part[:, n * GROUP : (n + 1) * GROUP] for n in range(2) for part in parts], axis=1
    )
    grads = dot_nt(rows, w_ref[:, width:])
    half = grads.shape[0] // 2
    put(left_ref, grads[:half])
    put(right_ref, grads[half:])


def halo_back(after, me, parts, shards):
    packs, span, _ = parts[0].shape
    width = shards[0].shape[1] // 3
    edge = lambda n: pl.BlockSpec((packs, HALF, 3 * GROUP), lambda i: (i, n, 0))
    return pl.pallas_call(
        ordered(halo_back_kernel, 9, after),
        grid=(1,),
        in_specs=[SMEM] + [edge(0)] * 2 + [edge(span // HALF - 1)] * 2
        + [ANY] * (4 + len(after)),
        out_specs=[per_pack(HALF, width, packs=packs)] * 2,
        out_shape=[jax.ShapeDtypeStruct((packs, HALF, width), BF16)] * 2,
        scratch_shapes=[pltpu.VMEM((width, 3 * width), BF16), pltpu.SemaphoreType.DMA((4,))],
        compiler_params=PARAMS,
        cost_estimate=cost(1.2, 6),
        name="halo_back",
    )(me, *parts, *parts, *shards, *after)


def own_back_kernel(me_ref, p0, p1, s0, s1, s2, s3, own_ref, w_ref, sems):
    copies = stage_weight(me_ref[0], (s0, s1, s2, s3), w_ref, sems)
    block = own_ref.shape[1]

    @pl.when(pl.program_id(0) == 0)
    def _():
        for copy in copies:
            copy.start()
        for copy in copies:
            copy.wait()

    own = slice(HALF, HALF + block)
    parts = [part[:, own, :].reshape(-1, part.shape[2]) for part in (p0, p1)]
    rows = jnp.concatenate(
        [part[:, n * GROUP : (n + 1) * GROUP] for n in range(3) for part in parts], axis=1
    )
    put(own_ref, dot_nt(rows, w_ref[...]))


def own_back(after, me, parts, shards):
    packs, span, _ = parts[0].shape
    block, width = span - 2 * HALF, shards[0].shape[1] // 3
    return pl.pallas_call(
        ordered(own_back_kernel, 7, after),
        grid=(packs // STEP,),
        in_specs=[SMEM] + [per_pack(span, 3 * GROUP, packs=STEP)] * 2
        + [ANY] * (4 + len(after)),
        out_specs=per_pack(block, width, packs=STEP),
        out_shape=jax.ShapeDtypeStruct((packs, block, width), BF16),
        scratch_shapes=[pltpu.VMEM((width, 3 * width), BF16), pltpu.SemaphoreType.DMA((4,))],
        compiler_params=PARAMS,
        cost_estimate=cost(5, 15),
        name="own_back",
    )(me, *parts, *shards, *after)


def finish_kernel(x_ref, own_ref, fl_ref, fr_ref, gm_ref, gain_ref, out_ref):
    block = x_ref.shape[1]
    normal, inverse = norm_of(x_ref[0].astype(F32))
    grad = own_ref[0].astype(F32)
    grad = jnp.concatenate(
        [
            grad[:HALF] + fl_ref[0].astype(F32),
            grad[HALF : block - HALF],
            grad[block - HALF :] + fr_ref[0].astype(F32),
        ],
        axis=0,
    )
    out_ref[0] = (gm_ref[0] + norm_back(grad, normal, inverse, gain_ref[...])).astype(BF16)


def finish(after, tokens, own, from_left, from_right, grad_middle, gain):
    packs, block, width = tokens.shape
    per_pack = lambda *dims: pl.BlockSpec((1,) + dims, lambda i: (i,) + (0,) * len(dims))
    return pl.pallas_call(
        ordered(finish_kernel, 6, after),
        grid=(packs,),
        in_specs=[
            per_pack(block, width),
            per_pack(block, width),
            per_pack(HALF, width),
            per_pack(HALF, width),
            per_pack(block, width),
            pl.BlockSpec((1, width), lambda i: (0, 0)),
        ]
        + [ANY] * len(after),
        out_specs=per_pack(block, width),
        out_shape=jax.ShapeDtypeStruct((packs, block, width), BF16),
        cost_estimate=pl.CostEstimate(flops=20_000_000, bytes_accessed=10_000_000, transcendentals=0),
        name="finish",
    )(tokens, own, from_left, from_right, grad_middle, gain, *after)


def tables(start, count):
    half_size = HEAD // 2
    freqs = jnp.power(THETA, -jnp.arange(half_size, dtype=F32) * (2.0 / HEAD))
    positions = (start + jnp.arange(count, dtype=jnp.int32)).astype(F32)
    angles = positions[:, None] * freqs[None, :]
    cos, sin = jnp.cos(angles), jnp.sin(angles)
    return (
        jnp.concatenate([cos, cos, cos, cos], axis=-1),
        jnp.concatenate([-sin, sin, -sin, sin], axis=-1),
    )


def weight_grad(left, right):
    return dot_tn(
        left.reshape(-1, left.shape[-1]), right.reshape(-1, right.shape[-1])
    ).astype(BF16)


def gain_grad(grad, weight, gain):
    return jnp.sum(grad * weight.astype(F32), axis=1) / gain.astype(F32)


def per_device(tokens, doc_begin, gain_attn, w_qkv, w_att_out, gain_mlp, w_in, w_down, cotangent):
    packs, block, width = tokens.shape
    me_w, me_c = lax.axis_index("wsh"), lax.axis_index("ctx")
    me = me_w.reshape(1).astype(jnp.int32)
    part = gain_attn.shape[0]

    row = jnp.zeros((16, w_qkv.shape[1]), BF16)
    row = lax.dynamic_update_slice(row, gain_attn[None], (0, me_w * part))
    row = lax.dynamic_update_slice(row, gain_mlp[None], (0, width + me_w * part))
    qkv = jnp.concatenate([w_qkv, row], axis=0)
    qkv_near, qkv_far = swap(qkv, "wsh", 1), swap(qkv, "wsh", 2)
    halo_left = shifted(tokens[:, block - HALF :], "ctx", 1)
    doc_rows = jnp.broadcast_to(doc_begin.astype(BF16)[:, :, None], (packs, 16, width))
    halo_right = shifted(jnp.concatenate([tokens[:, :HALF], doc_rows], axis=1), "ctx", -1)
    both = jnp.concatenate([w_att_out, w_down], axis=0)
    at_x, half_rows = me_c % 2, part // 2
    in_half = lax.dynamic_slice_in_dim(w_in, at_x * half_rows, half_rows, 0)
    qkv_far, halo_left, halo_right, in_half, both = lax.optimization_barrier(
        (qkv_far, halo_left, halo_right, in_half, both)
    )
    in_half = swap(in_half, "wsh", 2)
    both_far = swap(both, "wsh", 2)
    qkv_shards = (qkv, qkv_near, qkv_far, swap(qkv_far, "wsh", 1))
    gain_rows = sum(shard[part : part + 1].astype(F32) for shard in qkv_shards)
    gain_one, gain_two = gain_rows[:, :width], gain_rows[:, width : 2 * width]
    doc_right = halo_right[:, HALF, 0].astype(jnp.int32)
    left_ok = (doc_begin[:, 0] < me_c).astype(jnp.int32)
    right_ok = (
        (doc_right == doc_begin[:, 0]) & (me_c + 1 < lax.axis_size("ctx"))
    ).astype(jnp.int32)
    cos, sin = tables(me_c * block - HALF, block + 2 * HALF)


    q, kv, first_in = project(
        me, tokens, halo_left, halo_right, cos, sin, qkv_shards
    )
    in_half, q = lax.optimization_barrier((in_half, q))
    in_other = swap(in_half, "ctx", 1)
    both_near, in_near = swap(both, "wsh", 1), swap(w_in, "wsh", 1)
    probs, mixed = attend((), left_ok, right_ok, q, kv)
    both_far, in_half, in_other, both_near, in_near, mixed = lax.optimization_barrier(
        (both_far, in_half, in_other, both_near, in_near, mixed)
    )
    both_far_near = swap(both_far, "wsh", 1)
    in_far = joined(in_half, in_other, at_x, 0)
    in_far_near = swap(in_far, "wsh", 1)
    in_shards = (w_in, in_near, in_far, in_far_near)
    both_shards = (both, both_near, both_far, both_far_near)

    output, second_in, hidden, ggu, middle = hidden_layer(
        me, tokens, mixed, cotangent, gain_two, both_shards, in_shards
    )
    grad = weight_grad(second_in, ggu)
    sum_in = Reduction(grad, bits=(2, 1))
    sum_in.value, hidden = lax.optimization_barrier((sum_in.value, hidden))
    sum_in.begin_core()
    sum_both = Reduction(weight_grad(hidden, cotangent), bits=(2, 1))
    (sum_both.value,) = meet((sum_in,), sum_both.value)
    sum_in.end_core()
    sum_in.begin_side()
    sum_both.begin_core()
    low, gmix, grad_out = middle_back(
        (sum_in.value, sum_both.value),
        me, middle, ggu, cotangent, mixed, gain_two, both_shards, in_shards,
    )
    low, gmix, grad_out = meet((sum_both, sum_in), low, gmix, grad_out)
    sum_both.end_core()
    sum_in.end_side()
    sum_out = Reduction(grad_out)
    sum_out.begin_core()
    sum_out.end_core()
    sum_both.join(sum_out)
    depart(sum_in, sum_both)
    sum_both.begin_side()
    sum_in.begin_plane()
    back = lambda group, *after: attend_back(
        group, after, me, q, kv, probs, gmix, cos, sin, first_in
    )
    back_0, grad_0 = back(0, sum_in.value, sum_both.value)
    back_0, grad_0 = meet((sum_in, sum_both), back_0, grad_0)
    sum_in.end_plane()
    sum_both.end_side()
    sum_0 = Reduction(grad_0)
    sum_0.begin_core()
    sum_0.end_core()
    depart(sum_in, sum_both, sum_0)
    sum_0.begin_side()
    sum_in.begin_far()
    sum_both.begin_across()
    back_1, grad_1 = back(1, sum_in.value, sum_both.value, sum_0.value)
    back_1, grad_1 = meet((sum_in, sum_both, sum_0), back_1, grad_1)
    sum_in.end_far()
    sum_both.end_across()
    sum_0.end_side()
    sum_1 = Reduction(grad_1)
    sum_1.begin_core()
    depart(sum_in, sum_both, sum_0)
    sum_in.begin_spread()
    sum_1.end_core()
    sum_1.begin_side()
    sum_0.begin_across()
    sum_both.begin_near()
    parts = (back_0, back_1)
    to_left, to_right = halo_back(
        (sum_1.value, sum_in.value, sum_0.value, sum_both.value), me, parts, qkv_shards
    )
    to_left, to_right = meet((sum_0, sum_both, sum_in), to_left, to_right)
    sum_0.end_across()
    sum_both.end_near()
    sum_in.end_spread()
    depart(sum_0, sum_both, sum_in)
    sum_in.begin_last()
    sum_0.begin_near()
    from_right = shifted(to_left, "ctx", -1)
    from_left = shifted(to_right, "ctx", 1)
    own = own_back((sum_0.value, sum_both.value), me, parts, qkv_shards)
    own, from_left, from_right = meet((sum_0, sum_1, sum_in), own, from_left, from_right)
    sum_1.end_side()
    sum_0.end_near()
    depart(sum_0, sum_1, sum_both)
    sum_1.begin_plane()
    sum_0.begin_far()
    sum_both.begin_far()
    grad_tokens = finish(
        (sum_1.value, sum_0.value, sum_both.value),
        tokens, own, from_left, from_right, low, gain_one,
    )
    (grad_tokens,) = meet((sum_0, sum_1, sum_both), grad_tokens)
    sum_1.end_plane()
    sum_0.end_far()
    sum_both.end_far()
    depart(sum_0, sum_1, sum_both)
    sum_1.begin_far()
    sum_0.begin_spread()
    sum_both.begin_spread()
    meet((sum_0, sum_1, sum_both))
    sum_1.end_far()
    sum_0.end_spread()
    sum_both.end_spread()
    depart(sum_0, sum_1, sum_both)
    sum_1.begin_gather()
    sum_0.begin_last()
    sum_both.begin_last()
    meet((sum_0, sum_1, sum_both))
    grad_in = sum_in.end_last()
    grad_both = sum_both.end_last()
    pieces = [sum_0.end_last(), sum_1.end_gather()]
    grad_qkv = jnp.concatenate(
        [item[:, n * GROUP : (n + 1) * GROUP] for n in range(3) for item in pieces], axis=1
    )
    down = w_down.shape[0]
    return (
        output, grad_tokens, gain_grad(grad_qkv, w_qkv, gain_attn), grad_qkv, grad_both[down:],
        gain_grad(grad_in, w_in, gain_mlp), grad_in, grad_both[:down],
    )


def solution(mesh):
    return jax.shard_map(
        per_device,
        mesh=mesh,
        in_specs=(
            P("wsh", "ctx", None),
            P("wsh", "ctx"),
            P("wsh"),
            P("wsh", None),
            P("wsh", None),
            P("wsh"),
            P("wsh", None),
            P("wsh", None),
            P("wsh", "ctx", None),
        ),
        out_specs=(
            P("wsh", "ctx", None),
            P("wsh", "ctx", None),
            P("wsh"),
            P("wsh", None),
            P("wsh", None),
            P("wsh"),
            P("wsh", None),
            P("wsh", None),
        ),
        check_vma=False,
    )
```

```python
import functools
import math

import jax
import jax.numpy as jnp
from jax import lax
from jax.experimental import pallas as pl
from jax.experimental.pallas import tpu as pltpu
from jax.sharding import PartitionSpec as P

HEAD = 64
HALF = 64
EPS = 1e-05
THETA = 10000.0
MASKED = -1e30
PAIR = 2 * HEAD
QROWS = 128
WIN = QROWS + 2 * HALF
VMEM_BYTES = 56 * 1024 * 1024
STEP = 1

F32 = jnp.float32
BF16 = jnp.bfloat16


def dot_nn(left, right):
    return jnp.dot(left, right, preferred_element_type=F32)


def dot_nt(left, right):
    return lax.dot_general(left, right, (((1,), (1,)), ((), ())), preferred_element_type=F32)


def dot_tn(left, right):
    return lax.dot_general(left, right, (((0,), (0,)), ((), ())), preferred_element_type=F32)


def swap(value, axis, bit):
    peers = lax.axis_size(axis)
    return lax.ppermute(value, axis, [(i, i ^ bit) for i in range(peers)])


def shifted(value, axis, by):
    peers = lax.axis_size(axis)
    return lax.ppermute(value, axis, [(i, i + by) for i in range(peers) if 0 <= i + by < peers])


def pick(value, index, axis=0):
    return lax.dynamic_index_in_dim(value, index, axis, keepdims=False)


def added(kept, *received):
    total = kept.astype(F32)
    for item in received:
        total = total + item.astype(F32)
    return total.astype(BF16)


class Reduction:
    def __init__(self, grad, bits=(1, 2)):
        self.bits = bits
        self.me_w, self.me_c = lax.axis_index("wsh"), lax.axis_index("ctx")
        self.at_first, self.at_second = (self.me_c // bit % 2 for bit in bits)
        self.value = grad.reshape(2, 2, grad.shape[0] // 4, grad.shape[1])
        self.small = lax.axis_size("ctx") == 8
        self.got = ()

    def begin(self, send, axis, bit):
        self.got = (swap(send, axis, bit),)

    def begin_core(self):
        self.got = (swap(pick(self.value, 1 - self.me_w % 2, 1), "wsh", 1),)

    def end_core(self):
        self.value = added(pick(self.value, self.me_w % 2, 1), *self.got)
        return self.value

    def join(self, other):
        self.value = jnp.concatenate([self.value, other.value], axis=1)

    def begin_side(self):
        self.begin(pick(self.value, 1 - self.me_w // 2), "wsh", 2)

    def end_side(self):
        self.value = added(pick(self.value, self.me_w // 2), *self.got)
        self.half, self.chunk = self.value.shape[1] // 2, self.value.shape[0] // 2
        return self.value

    def halves(self, index):
        return lax.dynamic_slice_in_dim(self.value, index * self.half, self.half, 1)

    def chunks(self, index):
        return lax.dynamic_slice_in_dim(self.value, index * self.chunk, self.chunk, 0)

    def begin_across(self):
        self.got = ()
        if self.small:
            self.begin(self.halves(1 - self.at_first), "ctx", self.bits[0])

    def end_across(self):
        if self.small:
            self.value = added(self.halves(self.at_first), *self.got)
        return self.value

    def begin_near(self):
        self.got = ()
        if self.small:
            self.begin(self.chunks(1 - self.at_second), "ctx", self.bits[1])

    def end_near(self):
        if self.small:
            self.value = added(self.chunks(self.at_second), *self.got)
        return self.value

    def quarters(self, first, second):
        return lax.dynamic_slice(
            self.value, (second * self.chunk, first * self.half), (self.chunk, self.half)
        )

    def begin_plane(self):
        self.got = ()
        if self.small:
            first, second = self.bits
            self.got = tuple(
                swap(self.quarters(self.at_first ^ f, self.at_second ^ s), "ctx", f * first + s * second)
                for f, s in ((1, 1), (0, 1), (1, 0))
            )

    def end_plane(self):
        if self.small:
            self.value = added(self.quarters(self.at_first, self.at_second), *self.got)
        return self.value

    def begin_gather(self):
        self.got = ()
        if self.small:
            first, second = self.bits
            self.got = tuple(
                swap(self.value, "ctx", f * first + s * second) for f, s in ((1, 1), (0, 1), (1, 0))
            )

    def end_gather(self):
        if not self.small:
            return lax.psum(self.value.astype(F32), "ctx")
        across, second, first = self.got
        return joined(
            joined(self.value, second, self.at_second, 0),
            joined(first, across, self.at_second, 0),
            self.at_first,
            1,
        ).astype(F32)

    def begin_far(self):
        self.got = ()
        if self.small:
            self.begin(self.value, "ctx", 4)

    def end_far(self):
        if self.small:
            self.value = added(self.value, *self.got)
        return self.value

    def begin_spread(self):
        self.got = ()
        if self.small:
            self.begin(self.value, "ctx", self.bits[1])

    def end_spread(self):
        if self.small:
            self.value = joined(self.value, *self.got, self.at_second, 0)
        return self.value

    def begin_last(self):
        self.got = ()
        if self.small:
            self.begin(self.value, "ctx", self.bits[0])

    def end_last(self):
        if not self.small:
            return lax.psum(self.value.astype(F32), "ctx")
        return joined(self.value, *self.got, self.at_first, 1).astype(F32)


def meet(sums, *arrays):
    out = list(
        lax.optimization_barrier(sum((item.got for item in sums), ()) + arrays)
    )
    for item in sums:
        item.got, out = tuple(out[: len(item.got)]), out[len(item.got) :]
    return out


def depart(*sums):
    for item, value in zip(sums, lax.optimization_barrier(tuple(item.value for item in sums))):
        item.value = value


def joined(mine, other, place, axis):
    low = jnp.where(place == 0, mine, other)
    high = jnp.where(place == 0, other, mine)
    return jnp.concatenate([low, high], axis=axis)


def stage_weight(me, shards, scratch, sems, start=0):
    rows = scratch.shape[0] // 4
    return [
        pltpu.make_async_copy(
            shard.at[pl.ds(start, rows)], scratch.at[pl.ds(pl.multiple_of((me ^ k) * rows, rows), rows)], sems.at[k]
        )
        for k, shard in enumerate(shards)
    ]


def norm_of(values):
    average = jnp.mean(values, axis=-1, keepdims=True)
    centred = values - average
    inverse = lax.rsqrt(jnp.mean(centred * centred, axis=-1, keepdims=True) + EPS)
    return centred * inverse, inverse


def norm_back(incoming, normal, inverse, gain):
    scaled = incoming * gain
    return inverse * (
        scaled
        - jnp.mean(scaled, axis=-1, keepdims=True)
        - normal * jnp.mean(scaled * normal, axis=-1, keepdims=True)
    )


def head_lanes():
    lane = lax.broadcasted_iota(jnp.int32, (1, PAIR), 1)
    return lane, lane < HEAD


def turned(value, lane):
    ahead = pltpu.roll(value, PAIR - HEAD // 2, 1)
    behind = pltpu.roll(value, HEAD // 2, 1)
    return jnp.where(lane % HEAD < HEAD // 2, ahead, behind)


def stacked(value, first, scale):
    one = jnp.where(first, scale, 0.0).astype(BF16)
    two = jnp.where(first, 0.0, scale).astype(BF16)
    return jnp.concatenate([value * one, value * two], axis=0)


def per_pack(*dims, packs=1):
    return pl.BlockSpec((packs,) + dims, lambda i: (i,) + (0,) * len(dims))


def rows_of(ref):
    return ref[...].reshape(-1, ref.shape[-1])


def put(ref, value):
    ref[...] = value.astype(ref.dtype).reshape(ref.shape)


def fixed(*dims):
    return pl.BlockSpec(dims, lambda i: (0,) * len(dims))


def cost(gflops, megabytes):
    return pl.CostEstimate(
        flops=int(gflops * 1e8), bytes_accessed=int(megabytes * 1e5), transcendentals=0
    )


def ordered(kernel, count, after):
    return lambda *refs: kernel(*refs[:count], *refs[count + len(after) :])


SMEM = pl.BlockSpec(memory_space=pltpu.SMEM)
ANY = pl.BlockSpec(memory_space=pl.ANY)
PARAMS = pltpu.CompilerParams(vmem_limit_bytes=VMEM_BYTES)


def project_kernel(
    me_ref, x_ref, hl_ref, hr_ref, cos_ref, sin_ref, s0, s1, s2, s3,
    q_ref, kv_ref, first_ref, w_ref, gain_ref, sems, gain_sems,
):
    pack = pl.program_id(0)
    block = x_ref.shape[1]
    width = x_ref.shape[2]
    shards = (s0, s1, s2, s3)
    copies = stage_weight(me_ref[0], shards, w_ref, sems)
    gains = [
        pltpu.make_async_copy(
            shard.at[pl.ds(width // 4, 16), pl.ds(0, width)], gain_ref.at[n], gain_sems.at[n]
        )
        for n, shard in enumerate(shards)
    ]

    @pl.when(pack == 0)
    def _():
        for copy in gains + copies:
            copy.start()
        for copy in gains:
            copy.wait()

    values = jnp.concatenate([hl_ref[0], x_ref[0], hr_ref[0]], axis=0).astype(F32)
    normal, _ = norm_of(values)
    gain = jnp.sum(gain_ref[...].astype(F32), axis=0)[:1]
    first_ref[0] = (normal * gain).astype(BF16)
    lane, first = head_lanes()
    cos, sin = cos_ref[...], sin_ref[...]
    own = slice(HALF, HALF + block)
    step = 2 * PAIR

    @pl.when(pack == 0)
    def _():
        for copy in copies:
            copy.wait()

    for j in range(width // step):
        cols = slice(j * step, (j + 1) * step)
        q = dot_nn(first_ref[0, own, :], w_ref[:, cols])
        k = dot_nn(first_ref[0], w_ref[:, width + j * step : width + (j + 1) * step])
        v = dot_nn(first_ref[0], w_ref[:, 2 * width + j * step : 2 * width + (j + 1) * step])
        for i in range(2):
            part = slice(i * PAIR, (i + 1) * PAIR)
            base = j * step + i * PAIR
            qp, kp = q[:, part], k[:, part]
            q_ref[0, :, base : base + PAIR] = (
                qp * cos[own] + turned(qp, lane) * sin[own]
            ).astype(BF16)
            kv_ref[0, :, base : base + PAIR] = (kp * cos + turned(kp, lane) * sin).astype(BF16)
        kv_ref[0, :, width + j * step : width + (j + 1) * step] = v.astype(BF16)


def project(me, tokens, halo_left, halo_right, cos, sin, shards):
    packs, block, width = tokens.shape
    span = block + 2 * HALF
    return pl.pallas_call(
        project_kernel,
        grid=(packs,),
        in_specs=[SMEM, per_pack(block, width), per_pack(HALF, width), per_pack(HALF, width)]
        + [fixed(span, PAIR), fixed(span, PAIR)]
        + [ANY] * 4,
        out_specs=[per_pack(block, width), per_pack(span, 2 * width), per_pack(span, width)],
        out_shape=[
            jax.ShapeDtypeStruct((packs, block, width), BF16),
            jax.ShapeDtypeStruct((packs, span, 2 * width), BF16),
            jax.ShapeDtypeStruct((packs, span, width), BF16),
        ],
        scratch_shapes=[
            pltpu.VMEM((width, 3 * width), BF16),
            pltpu.VMEM((4, 16, width), BF16),
            pltpu.SemaphoreType.DMA((4,)),
            pltpu.SemaphoreType.DMA((4,)),
        ],
        compiler_params=PARAMS,
        cost_estimate=cost(5, 15),
        name="project",
    )(me, tokens, halo_left, halo_right, cos, sin, *shards)


def attend_kernel(left_ok, right_ok, q_ref, kv_ref, probs_ref, mixed_ref):
    pack = pl.program_id(0)
    block, width = q_ref.shape[1], q_ref.shape[2]
    _, first = head_lanes()
    row = lax.broadcasted_iota(jnp.int32, (QROWS, WIN), 0)
    col = lax.broadcasted_iota(jnp.int32, (QROWS, WIN), 1)
    near = (col >= row) & (col <= row + 2 * HALF)
    blocks = block // QROWS
    biases = []
    for b in range(blocks):
        allowed = near
        if b == 0:
            allowed = allowed & ((col >= HALF) | (left_ok[pack] > 0))
        if b == blocks - 1:
            allowed = allowed & ((col < WIN - HALF) | (right_ok[pack] > 0))
        bias = jnp.where(allowed, 0.0, MASKED)
        biases.append(jnp.concatenate([bias, bias], axis=0))
    rows = lambda b: slice(b * QROWS, (b + 1) * QROWS)
    window = lambda b: slice(b * QROWS, b * QROWS + WIN)
    cols = lambda p: slice(p * PAIR, (p + 1) * PAIR)
    for start in range(0, width // PAIR, 2):
        tiles = [(p, b) for p in range(start, start + 2) for b in range(blocks)]
        scores = [
            dot_nt(
                stacked(q_ref[0, rows(b), cols(p)], first, HEAD ** -0.5),
                kv_ref[0, window(b), cols(p)],
            )
            + biases[b]
            for p, b in tiles
        ]
        tops = [jnp.max(item, axis=-1, keepdims=True) for item in scores]
        powers = [jnp.exp(item - top) for item, top in zip(scores, tops)]
        sums = [1.0 / jnp.sum(item, axis=-1, keepdims=True) for item in powers]
        probs = [(item * one).astype(BF16) for item, one in zip(powers, sums)]
        for (p, b), item in zip(tiles, probs):
            probs_ref[0, p, b] = item
            out = dot_nn(item, kv_ref[0, window(b), width + p * PAIR : width + (p + 1) * PAIR])
            mixed_ref[0, rows(b), cols(p)] = jnp.where(first, out[:QROWS], out[QROWS:]).astype(BF16)


def attend(after, left_ok, right_ok, q, kv):
    packs, block, width = q.shape
    pairs, blocks = width // PAIR, block // QROWS
    return pl.pallas_call(
        ordered(attend_kernel, 4, after),
        grid=(packs,),
        in_specs=[SMEM, SMEM, per_pack(block, width), per_pack(block + 2 * HALF, 2 * width)]
        + [ANY] * len(after),
        out_specs=[per_pack(pairs, blocks, 2 * QROWS, WIN), per_pack(block, width)],
        out_shape=[
            jax.ShapeDtypeStruct((packs, pairs, blocks, 2 * QROWS, WIN), BF16),
            jax.ShapeDtypeStruct((packs, block, width), BF16),
        ],
        compiler_params=PARAMS,
        cost_estimate=cost(10, 15),
        name="attend",
    )(left_ok, right_ok, q, kv, *after)


def hidden_kernel(
    me_ref, x_ref, mixed_ref, up_ref, gain_ref, o0, o1, o2, o3, i0, i1, i2, i3,
    out_ref, second_ref, hidden_ref, ggu_ref, middle_ref,
    wo_ref, wi_ref, wd_ref, sems,
):
    tile = pl.program_id(0)
    ff = wd_ref.shape[0]
    both = (o0, o1, o2, o3)
    copies = [
        stage_weight(me_ref[0], both, wo_ref, sems.at[0]),
        stage_weight(me_ref[0], (i0, i1, i2, i3), wi_ref, sems.at[1]),
        stage_weight(me_ref[0], both, wd_ref, sems.at[2], wo_ref.shape[0] // 4),
    ]

    @pl.when(tile == 0)
    def _():
        for group in copies:
            for copy in group:
                copy.start()
        for copy in copies[0]:
            copy.wait()

    middle = rows_of(x_ref).astype(F32) + dot_nn(rows_of(mixed_ref), wo_ref[...])
    put(middle_ref, middle)
    normal, _ = norm_of(middle)
    second = (normal * gain_ref[...]).astype(BF16)
    put(second_ref, second)
    upstream = rows_of(up_ref)

    @pl.when(tile == 0)
    def _():
        for group in copies[1:]:
            for copy in group:
                copy.wait()

    step = ff
    result = middle
    for j in range(ff // step):
        cols = slice(j * step, (j + 1) * step)
        ups = slice(ff + j * step, ff + (j + 1) * step)
        gate = dot_nn(second, wi_ref[:, cols])
        up = dot_nn(second, wi_ref[:, ups])
        grad_hidden = dot_nt(upstream, wd_ref[cols, :])
        cumulative = 0.5 + 0.5 * lax.erf(gate * (0.5 ** 0.5))
        activated = gate * cumulative
        density = jnp.exp(-0.5 * gate * gate) * (1.0 / math.sqrt(2.0 * math.pi))
        hidden = (activated * up).astype(BF16)
        put(hidden_ref.at[:, :, cols], hidden)
        put(ggu_ref.at[:, :, cols], grad_hidden * up * (cumulative + gate * density))
        put(ggu_ref.at[:, :, ups], grad_hidden * activated)
        result = result + dot_nn(hidden, wd_ref[cols, :])
    put(out_ref, result)


def hidden_layer(me, tokens, mixed, upstream, gain, both_shards, in_shards):
    packs, block, width = tokens.shape
    ff = in_shards[0].shape[1] // 2
    shape = lambda dtype, *dims: jax.ShapeDtypeStruct((packs, block) + dims, dtype)
    return pl.pallas_call(
        hidden_kernel,
        grid=(packs // STEP,),
        in_specs=[SMEM] + [per_pack(block, width, packs=STEP)] * 3 + [fixed(1, width)] + [ANY] * 8,
        out_specs=[
            per_pack(block, width, packs=STEP),
            per_pack(block, width, packs=STEP),
            per_pack(block, ff, packs=STEP),
            per_pack(block, 2 * ff, packs=STEP),
            per_pack(block, width, packs=STEP),
        ],
        out_shape=[
            shape(BF16, width),
            shape(BF16, width),
            shape(BF16, ff),
            shape(BF16, 2 * ff),
            shape(BF16, width),
        ],
        scratch_shapes=[
            pltpu.VMEM((width, width), BF16),
            pltpu.VMEM((width, 2 * ff), BF16),
            pltpu.VMEM((ff, width), BF16),
            pltpu.SemaphoreType.DMA((3, 4)),
        ],
        compiler_params=PARAMS,
        cost_estimate=cost(16, 25),
        name="hidden_layer",
    )(me, tokens, mixed, upstream, gain, *both_shards, *in_shards)


def middle_kernel(
    me_ref, middle_ref, ggu_ref, up_ref, mixed_ref, gain_ref, o0, o1, o2, o3, i0, i1, i2, i3,
    low_ref, gmix_ref, gout_ref, wo_ref, wi_ref, total_ref, sems,
):
    tile = pl.program_id(0)
    copies = [
        stage_weight(me_ref[0], group, scratch, sems.at[n])
        for n, (group, scratch) in enumerate(
            (((o0, o1, o2, o3), wo_ref), ((i0, i1, i2, i3), wi_ref))
        )
    ]

    @pl.when(tile == 0)
    def _():
        for group in copies:
            for copy in group:
                copy.start()
        total_ref[...] = jnp.zeros_like(total_ref)

    normal, inverse = norm_of(rows_of(middle_ref).astype(F32))

    @pl.when(tile == 0)
    def _():
        for group in copies:
            for copy in group:
                copy.wait()

    grad_second = dot_nt(rows_of(ggu_ref), wi_ref[...])
    grad_middle = rows_of(up_ref).astype(F32) + norm_back(grad_second, normal, inverse, gain_ref[...])
    low = grad_middle.astype(BF16)
    put(low_ref, low)
    put(gmix_ref, dot_nt(low, wo_ref[...]))
    total_ref[...] += dot_tn(rows_of(mixed_ref), low)

    @pl.when(tile == pl.num_programs(0) - 1)
    def _():
        gout_ref[...] = total_ref[...].astype(BF16)


def middle_back(after, me, middle, ggu, upstream, mixed, gain, out_shards, in_shards):
    packs, block, width = middle.shape
    wide = ggu.shape[2]
    shape = lambda dtype, *dims: jax.ShapeDtypeStruct((packs, block) + dims, dtype)
    return pl.pallas_call(
        ordered(middle_kernel, 14, after),
        grid=(packs // STEP,),
        in_specs=[SMEM, per_pack(block, width, packs=STEP), per_pack(block, wide, packs=STEP)]
        + [per_pack(block, width, packs=STEP)] * 2
        + [fixed(1, width)]
        + [ANY] * (8 + len(after)),
        out_specs=[per_pack(block, width, packs=STEP)] * 2 + [fixed(width, width)],
        out_shape=[
            shape(BF16, width),
            shape(BF16, width),
            jax.ShapeDtypeStruct((width, width), BF16),
        ],
        scratch_shapes=[
            pltpu.VMEM((width, width), BF16),
            pltpu.VMEM((width, wide), BF16),
            pltpu.VMEM((width, width), F32),
            pltpu.SemaphoreType.DMA((2, 4)),
        ],
        compiler_params=PARAMS,
        cost_estimate=cost(8, 20),
        name="middle_back",
    )(me, middle, ggu, upstream, mixed, gain, *out_shards, *in_shards, *after)


GROUP = 3 * PAIR


def attend_back_kernel(
    me_ref, q_ref, k_ref, v_ref, probs_ref, gmix_ref, cos_ref, sin_ref, first_ref,
    dqkv_ref, grad_ref, all_ref,
):
    block = q_ref.shape[1]
    lane, first = head_lanes()
    cos, sin = cos_ref[...], -sin_ref[...]
    own = slice(HALF, HALF + block)
    dqkv_ref[0, :HALF, :GROUP] = jnp.zeros((HALF, GROUP), BF16)
    dqkv_ref[0, HALF + block :, :GROUP] = jnp.zeros((HALF, GROUP), BF16)
    for p in range(GROUP // PAIR):
        cols = slice(p * PAIR, (p + 1) * PAIR)
        blocks = range(block // QROWS)
        rows = [slice(b * QROWS, (b + 1) * QROWS) for b in blocks]
        window = [slice(b * QROWS, b * QROWS + WIN) for b in blocks]
        do2 = [stacked(gmix_ref[0, rows[b], cols], first, 1.0) for b in blocks]
        q2 = [stacked(q_ref[0, rows[b], cols], first, HEAD ** -0.5) for b in blocks]
        dprobs = [dot_nt(do2[b], v_ref[0, window[b], cols]) for b in blocks]
        dvs = [dot_tn(probs_ref[0, p, b], do2[b]) for b in blocks]
        wide = [probs_ref[0, p, b].astype(F32) for b in blocks]
        inner = [jnp.sum(dprobs[b] * wide[b], axis=-1, keepdims=True) for b in blocks]
        ds = [(wide[b] * (dprobs[b] - inner[b])).astype(BF16) for b in blocks]
        dq2 = [dot_nn(ds[b], k_ref[0, window[b], cols]) for b in blocks]
        dqs = [jnp.where(first, d[:QROWS], d[QROWS:]) * (HEAD ** -0.5) for d in dq2]
        dks = [dot_tn(ds[b], q2[b]) for b in blocks]
        dq = jnp.concatenate(dqs, axis=0)
        over = WIN - QROWS
        merge = lambda a, b: jnp.concatenate([a[:QROWS], a[QROWS:] + b[:over], b[over:]], axis=0)
        dk, dv = merge(*dks), merge(*dvs)
        at = lambda n: slice(n * GROUP + p * PAIR, n * GROUP + (p + 1) * PAIR)
        dqkv_ref[0, own, at(0)] = (dq * cos[own] + turned(dq, lane) * sin[own]).astype(BF16)
        dqkv_ref[0, :, at(1)] = (dk * cos + turned(dk, lane) * sin).astype(BF16)
        dqkv_ref[0, :, at(2)] = dv.astype(BF16)

    all_ref[pl.program_id(0)] = dqkv_ref[0]

    @pl.when(pl.program_id(0) == pl.num_programs(0) - 1)
    def _():
        for n in range(3):
            part = slice(n * GROUP, (n + 1) * GROUP)
            right = all_ref[:, :, part].reshape(-1, GROUP)
            grad_ref[:, part] = dot_tn(rows_of(first_ref), right).astype(BF16)


def attend_back(group, after, me, q, kv, probs, gmix, cos, sin, first_in):
    packs, block, width = q.shape
    span = block + 2 * HALF
    blocks, groups = block // QROWS, width // GROUP
    cols = lambda rows, g: pl.BlockSpec((1, rows, GROUP), lambda i: (i, 0, g))
    return pl.pallas_call(
        ordered(attend_back_kernel, 9, after),
        grid=(packs,),
        in_specs=[
            SMEM,
            cols(block, group),
            cols(span, group),
            cols(span, groups + group),
            pl.BlockSpec(
                (1, GROUP // PAIR, blocks, 2 * QROWS, WIN), lambda i: (i, group, 0, 0, 0)
            ),
            cols(block, group),
            fixed(span, PAIR),
            fixed(span, PAIR),
            fixed(packs, span, width),
        ]
        + [ANY] * len(after),
        out_specs=[per_pack(span, 3 * GROUP), fixed(width, 3 * GROUP)],
        out_shape=[
            jax.ShapeDtypeStruct((packs, span, 3 * GROUP), BF16),
            jax.ShapeDtypeStruct((width, 3 * GROUP), BF16),
        ],
        scratch_shapes=[pltpu.VMEM((packs, span, 3 * GROUP), BF16)],
        compiler_params=PARAMS,
        cost_estimate=cost(8, 10),
        name="attend_back",
    )(me, q, kv, kv, probs, gmix, cos, sin, first_in, *after)


def halo_back_kernel(
    me_ref, l0, l1, r0, r1, s0, s1, s2, s3, left_ref, right_ref, w_ref, sems
):
    copies = stage_weight(me_ref[0], (s0, s1, s2, s3), w_ref, sems)
    width = left_ref.shape[2]

    @pl.when(pl.program_id(0) == 0)
    def _():
        for copy in copies:
            copy.start()
        for copy in copies:
            copy.wait()

    parts = [
        jnp.concatenate([rows_of(left)[:, GROUP:], rows_of(right)[:, GROUP:]], axis=0)
        for left, right in ((l0, r0), (l1, r1))
    ]
    rows = jnp.concatenate(
        [part[:, n * GROUP : (n + 1) * GROUP] for n in range(2) for part in parts], axis=1
    )
    grads = dot_nt(rows, w_ref[:, width:])
    half = grads.shape[0] // 2
    put(left_ref, grads[:half])
    put(right_ref, grads[half:])


def halo_back(after, me, parts, shards):
    packs, span, _ = parts[0].shape
    width = shards[0].shape[1] // 3
    edge = lambda n: pl.BlockSpec((packs, HALF, 3 * GROUP), lambda i: (i, n, 0))
    return pl.pallas_call(
        ordered(halo_back_kernel, 9, after),
        grid=(1,),
        in_specs=[SMEM] + [edge(0)] * 2 + [edge(span // HALF - 1)] * 2
        + [ANY] * (4 + len(after)),
        out_specs=[per_pack(HALF, width, packs=packs)] * 2,
        out_shape=[jax.ShapeDtypeStruct((packs, HALF, width), BF16)] * 2,
        scratch_shapes=[pltpu.VMEM((width, 3 * width), BF16), pltpu.SemaphoreType.DMA((4,))],
        compiler_params=PARAMS,
        cost_estimate=cost(1.2, 6),
        name="halo_back",
    )(me, *parts, *parts, *shards, *after)


def own_back_kernel(me_ref, p0, p1, s0, s1, s2, s3, own_ref, w_ref, sems):
    copies = stage_weight(me_ref[0], (s0, s1, s2, s3), w_ref, sems)
    block = own_ref.shape[1]

    @pl.when(pl.program_id(0) == 0)
    def _():
        for copy in copies:
            copy.start()
        for copy in copies:
            copy.wait()

    own = slice(HALF, HALF + block)
    parts = [part[:, own, :].reshape(-1, part.shape[2]) for part in (p0, p1)]
    rows = jnp.concatenate(
        [part[:, n * GROUP : (n + 1) * GROUP] for n in range(3) for part in parts], axis=1
    )
    put(own_ref, dot_nt(rows, w_ref[...]))


def own_back(after, me, parts, shards):
    packs, span, _ = parts[0].shape
    block, width = span - 2 * HALF, shards[0].shape[1] // 3
    return pl.pallas_call(
        ordered(own_back_kernel, 7, after),
        grid=(packs // STEP,),
        in_specs=[SMEM] + [per_pack(span, 3 * GROUP, packs=STEP)] * 2
        + [ANY] * (4 + len(after)),
        out_specs=per_pack(block, width, packs=STEP),
        out_shape=jax.ShapeDtypeStruct((packs, block, width), BF16),
        scratch_shapes=[pltpu.VMEM((width, 3 * width), BF16), pltpu.SemaphoreType.DMA((4,))],
        compiler_params=PARAMS,
        cost_estimate=cost(5, 15),
        name="own_back",
    )(me, *parts, *shards, *after)


def finish_kernel(x_ref, own_ref, fl_ref, fr_ref, gm_ref, gain_ref, out_ref):
    block = x_ref.shape[1]
    normal, inverse = norm_of(x_ref[0].astype(F32))
    grad = own_ref[0].astype(F32)
    grad = jnp.concatenate(
        [
            grad[:HALF] + fl_ref[0].astype(F32),
            grad[HALF : block - HALF],
            grad[block - HALF :] + fr_ref[0].astype(F32),
        ],
        axis=0,
    )
    out_ref[0] = (gm_ref[0] + norm_back(grad, normal, inverse, gain_ref[...])).astype(BF16)


def finish(after, tokens, own, from_left, from_right, grad_middle, gain):
    packs, block, width = tokens.shape
    per_pack = lambda *dims: pl.BlockSpec((1,) + dims, lambda i: (i,) + (0,) * len(dims))
    return pl.pallas_call(
        ordered(finish_kernel, 6, after),
        grid=(packs,),
        in_specs=[
            per_pack(block, width),
            per_pack(block, width),
            per_pack(HALF, width),
            per_pack(HALF, width),
            per_pack(block, width),
            pl.BlockSpec((1, width), lambda i: (0, 0)),
        ]
        + [ANY] * len(after),
        out_specs=per_pack(block, width),
        out_shape=jax.ShapeDtypeStruct((packs, block, width), BF16),
        cost_estimate=pl.CostEstimate(flops=20_000_000, bytes_accessed=10_000_000, transcendentals=0),
        name="finish",
    )(tokens, own, from_left, from_right, grad_middle, gain, *after)


def tables(start, count):
    half_size = HEAD // 2
    freqs = jnp.power(THETA, -jnp.arange(half_size, dtype=F32) * (2.0 / HEAD))
    positions = (start + jnp.arange(count, dtype=jnp.int32)).astype(F32)
    angles = positions[:, None] * freqs[None, :]
    cos, sin = jnp.cos(angles), jnp.sin(angles)
    return (
        jnp.concatenate([cos, cos, cos, cos], axis=-1),
        jnp.concatenate([-sin, sin, -sin, sin], axis=-1),
    )


def weight_grad(left, right):
    return dot_tn(
        left.reshape(-1, left.shape[-1]), right.reshape(-1, right.shape[-1])
    ).astype(BF16)


def gain_grad(grad, weight, gain):
    return jnp.sum(grad * weight.astype(F32), axis=1) / gain.astype(F32)


def per_device(tokens, doc_begin, gain_attn, w_qkv, w_att_out, gain_mlp, w_in, w_down, cotangent):
    packs, block, width = tokens.shape
    me_w, me_c = lax.axis_index("wsh"), lax.axis_index("ctx")
    me = me_w.reshape(1).astype(jnp.int32)
    part = gain_attn.shape[0]

    row = jnp.zeros((16, w_qkv.shape[1]), BF16)
    row = lax.dynamic_update_slice(row, gain_attn[None], (0, me_w * part))
    row = lax.dynamic_update_slice(row, gain_mlp[None], (0, width + me_w * part))
    qkv = jnp.concatenate([w_qkv, row], axis=0)
    qkv_near, qkv_far = swap(qkv, "wsh", 1), swap(qkv, "wsh", 2)
    halo_left = shifted(tokens[:, block - HALF :], "ctx", 1)
    doc_rows = jnp.broadcast_to(doc_begin.astype(BF16)[:, :, None], (packs, 16, width))
    halo_right = shifted(jnp.concatenate([tokens[:, :HALF], doc_rows], axis=1), "ctx", -1)
    both = jnp.concatenate([w_att_out, w_down], axis=0)
    at_x, half_rows = me_c % 2, part // 2
    in_half = lax.dynamic_slice_in_dim(w_in, at_x * half_rows, half_rows, 0)
    qkv_far, halo_left, halo_right, in_half, both = lax.optimization_barrier(
        (qkv_far, halo_left, halo_right, in_half, both)
    )
    in_half = swap(in_half, "wsh", 2)
    both_far = swap(both, "wsh", 2)
    qkv_shards = (qkv, qkv_near, qkv_far, swap(qkv_far, "wsh", 1))
    gain_rows = sum(shard[part : part + 1].astype(F32) for shard in qkv_shards)
    gain_one, gain_two = gain_rows[:, :width], gain_rows[:, width : 2 * width]
    doc_right = halo_right[:, HALF, 0].astype(jnp.int32)
    left_ok = (doc_begin[:, 0] < me_c).astype(jnp.int32)
    right_ok = (
        (doc_right == doc_begin[:, 0]) & (me_c + 1 < lax.axis_size("ctx"))
    ).astype(jnp.int32)
    cos, sin = tables(me_c * block - HALF, block + 2 * HALF)


    q, kv, first_in = project(
        me, tokens, halo_left, halo_right, cos, sin, qkv_shards
    )
    in_half, q = lax.optimization_barrier((in_half, q))
    in_other = swap(in_half, "ctx", 1)
    both_near, in_near = swap(both, "wsh", 1), swap(w_in, "wsh", 1)
    probs, mixed = attend((), left_ok, right_ok, q, kv)
    both_far, in_half, in_other, both_near, in_near, mixed = lax.optimization_barrier(
        (both_far, in_half, in_other, both_near, in_near, mixed)
    )
    both_far_near = swap(both_far, "wsh", 1)
    in_far = joined(in_half, in_other, at_x, 0)
    in_far_near = swap(in_far, "wsh", 1)
    in_shards = (w_in, in_near, in_far, in_far_near)
    both_shards = (both, both_near, both_far, both_far_near)

    output, second_in, hidden, ggu, middle = hidden_layer(
        me, tokens, mixed, cotangent, gain_two, both_shards, in_shards
    )
    grad = weight_grad(second_in, ggu)
    sum_in = Reduction(grad, bits=(2, 1))
    sum_in.value, hidden = lax.optimization_barrier((sum_in.value, hidden))
    sum_in.begin_core()
    sum_both = Reduction(weight_grad(hidden, cotangent), bits=(2, 1))
    (sum_both.value,) = meet((sum_in,), sum_both.value)
    sum_in.end_core()
    sum_in.begin_side()
    sum_both.begin_core()
    low, gmix, grad_out = middle_back(
        (sum_in.value, sum_both.value),
        me, middle, ggu, cotangent, mixed, gain_two, both_shards, in_shards,
    )
    low, gmix, grad_out = meet((sum_both, sum_in), low, gmix, grad_out)
    sum_both.end_core()
    sum_in.end_side()
    sum_out = Reduction(grad_out)
    sum_out.begin_core()
    sum_out.end_core()
    sum_both.join(sum_out)
    depart(sum_in, sum_both)
    sum_both.begin_side()
    sum_in.begin_plane()
    back = lambda group, *after: attend_back(
        group, after, me, q, kv, probs, gmix, cos, sin, first_in
    )
    back_0, grad_0 = back(0, sum_in.value, sum_both.value)
    back_0, grad_0 = meet((sum_in, sum_both), back_0, grad_0)
    sum_in.end_plane()
    sum_both.end_side()
    sum_0 = Reduction(grad_0)
    sum_0.begin_core()
    sum_0.end_core()
    depart(sum_in, sum_both, sum_0)
    sum_0.begin_side()
    sum_in.begin_far()
    sum_both.begin_across()
    back_1, grad_1 = back(1, sum_in.value, sum_both.value, sum_0.value)
    back_1, grad_1 = meet((sum_in, sum_both, sum_0), back_1, grad_1)
    sum_in.end_far()
    sum_both.end_across()
    sum_0.end_side()
    sum_1 = Reduction(grad_1)
    sum_1.begin_core()
    depart(sum_in, sum_both, sum_0)
    sum_in.begin_spread()
    sum_1.end_core()
    sum_1.begin_side()
    sum_0.begin_across()
    sum_both.begin_near()
    parts = (back_0, back_1)
    to_left, to_right = halo_back(
        (sum_1.value, sum_in.value, sum_0.value, sum_both.value), me, parts, qkv_shards
    )
    to_left, to_right = meet((sum_0, sum_both, sum_in), to_left, to_right)
    sum_0.end_across()
    sum_both.end_near()
    sum_in.end_spread()
    depart(sum_0, sum_both, sum_in)
    sum_in.begin_last()
    sum_0.begin_near()
    from_right = shifted(to_left, "ctx", -1)
    from_left = shifted(to_right, "ctx", 1)
    own = own_back((sum_0.value, sum_both.value), me, parts, qkv_shards)
    own, from_left, from_right = meet((sum_0, sum_1, sum_in), own, from_left, from_right)
    sum_1.end_side()
    sum_0.end_near()
    depart(sum_0, sum_1, sum_both)
    sum_1.begin_plane()
    sum_0.begin_far()
    sum_both.begin_far()
    grad_tokens = finish(
        (sum_1.value, sum_0.value, sum_both.value),
        tokens, own, from_left, from_right, low, gain_one,
    )
    (grad_tokens,) = meet((sum_0, sum_1, sum_both), grad_tokens)
    sum_1.end_plane()
    sum_0.end_far()
    sum_both.end_far()
    depart(sum_0, sum_1, sum_both)
    sum_1.begin_far()
    sum_0.begin_spread()
    sum_both.begin_spread()
    meet((sum_0, sum_1, sum_both))
    sum_1.end_far()
    sum_0.end_spread()
    sum_both.end_spread()
    depart(sum_0, sum_1, sum_both)
    sum_1.begin_gather()
    sum_0.begin_last()
    sum_both.begin_last()
    meet((sum_0, sum_1, sum_both))
    grad_in = sum_in.end_last()
    grad_both = sum_both.end_last()
    pieces = [sum_0.end_last(), sum_1.end_gather()]
    grad_qkv = jnp.concatenate(
        [item[:, n * GROUP : (n + 1) * GROUP] for n in range(3) for item in pieces], axis=1
    )
    down = w_down.shape[0]
    return (
        output, grad_tokens, gain_grad(grad_qkv, w_qkv, gain_attn), grad_qkv, grad_both[down:],
        gain_grad(grad_in, w_in, gain_mlp), grad_in, grad_both[:down],
    )


def solution(mesh):
    return jax.shard_map(
        per_device,
        mesh=mesh,
        in_specs=(
            P("wsh", "ctx", None),
            P("wsh", "ctx"),
            P("wsh"),
            P("wsh", None),
            P("wsh", None),
            P("wsh"),
            P("wsh", None),
            P("wsh", None),
            P("wsh", "ctx", None),
        ),
        out_specs=(
            P("wsh", "ctx", None),
            P("wsh", "ctx", None),
            P("wsh"),
            P("wsh", None),
            P("wsh", None),
            P("wsh"),
            P("wsh", None),
            P("wsh", None),
        ),
        check_vma=False,
    )
```

```python
import functools
import math

import jax
import jax.numpy as jnp
from jax import lax
from jax.experimental import pallas as pl
from jax.experimental.pallas import tpu as pltpu
from jax.sharding import PartitionSpec as P

HEAD = 64
HALF = 64
EPS = 1e-05
THETA = 10000.0
MASKED = -1e30
PAIR = 2 * HEAD
QROWS = 128
WIN = QROWS + 2 * HALF
VMEM_BYTES = 56 * 1024 * 1024
STEP = 1

F32 = jnp.float32
BF16 = jnp.bfloat16


def dot_nn(left, right):
    return jnp.dot(left, right, preferred_element_type=F32)


def dot_nt(left, right):
    return lax.dot_general(left, right, (((1,), (1,)), ((), ())), preferred_element_type=F32)


def dot_tn(left, right):
    return lax.dot_general(left, right, (((0,), (0,)), ((), ())), preferred_element_type=F32)


def swap(value, axis, bit):
    peers = lax.axis_size(axis)
    return lax.ppermute(value, axis, [(i, i ^ bit) for i in range(peers)])


def shifted(value, axis, by):
    peers = lax.axis_size(axis)
    return lax.ppermute(value, axis, [(i, i + by) for i in range(peers) if 0 <= i + by < peers])


def pick(value, index, axis=0):
    return lax.dynamic_index_in_dim(value, index, axis, keepdims=False)


def added(kept, *received):
    total = kept.astype(F32)
    for item in received:
        total = total + item.astype(F32)
    return total.astype(BF16)


class Reduction:
    def __init__(self, grad, bits=(1, 2)):
        self.bits = bits
        self.me_w, self.me_c = lax.axis_index("wsh"), lax.axis_index("ctx")
        self.at_first, self.at_second = (self.me_c // bit % 2 for bit in bits)
        self.value = grad.reshape(2, 2, grad.shape[0] // 4, grad.shape[1])
        self.small = lax.axis_size("ctx") == 8
        self.got = ()

    def begin(self, send, axis, bit):
        self.got = (swap(send, axis, bit),)

    def begin_core(self):
        self.got = (swap(pick(self.value, 1 - self.me_w % 2, 1), "wsh", 1),)

    def end_core(self):
        self.value = added(pick(self.value, self.me_w % 2, 1), *self.got)
        return self.value

    def join(self, other):
        self.value = jnp.concatenate([self.value, other.value], axis=1)

    def begin_side(self):
        self.begin(pick(self.value, 1 - self.me_w // 2), "wsh", 2)

    def end_side(self):
        self.value = added(pick(self.value, self.me_w // 2), *self.got)
        self.half, self.chunk = self.value.shape[1] // 2, self.value.shape[0] // 2
        return self.value

    def halves(self, index):
        return lax.dynamic_slice_in_dim(self.value, index * self.half, self.half, 1)

    def chunks(self, index):
        return lax.dynamic_slice_in_dim(self.value, index * self.chunk, self.chunk, 0)

    def begin_across(self):
        self.got = ()
        if self.small:
            self.begin(self.halves(1 - self.at_first), "ctx", self.bits[0])

    def end_across(self):
        if self.small:
            self.value = added(self.halves(self.at_first), *self.got)
        return self.value

    def begin_near(self):
        self.got = ()
        if self.small:
            self.begin(self.chunks(1 - self.at_second), "ctx", self.bits[1])

    def end_near(self):
        if self.small:
            self.value = added(self.chunks(self.at_second), *self.got)
        return self.value

    def quarters(self, first, second):
        return lax.dynamic_slice(
            self.value, (second * self.chunk, first * self.half), (self.chunk, self.half)
        )

    def begin_plane(self):
        self.got = ()
        if self.small:
            first, second = self.bits
            self.got = tuple(
                swap(self.quarters(self.at_first ^ f, self.at_second ^ s), "ctx", f * first + s * second)
                for f, s in ((1, 1), (0, 1), (1, 0))
            )

    def end_plane(self):
        if self.small:
            self.value = added(self.quarters(self.at_first, self.at_second), *self.got)
        return self.value

    def begin_gather(self):
        self.got = ()
        if self.small:
            first, second = self.bits
            self.got = tuple(
                swap(self.value, "ctx", f * first + s * second) for f, s in ((1, 1), (0, 1), (1, 0))
            )

    def end_gather(self):
        if not self.small:
            return lax.psum(self.value.astype(F32), "ctx")
        across, second, first = self.got
        return joined(
            joined(self.value, second, self.at_second, 0),
            joined(first, across, self.at_second, 0),
            self.at_first,
            1,
        ).astype(F32)

    def begin_far(self):
        self.got = ()
        if self.small:
            self.begin(self.value, "ctx", 4)

    def end_far(self):
        if self.small:
            self.value = added(self.value, *self.got)
        return self.value

    def begin_spread(self):
        self.got = ()
        if self.small:
            self.begin(self.value, "ctx", self.bits[1])

    def end_spread(self):
        if self.small:
            self.value = joined(self.value, *self.got, self.at_second, 0)
        return self.value

    def begin_last(self):
        self.got = ()
        if self.small:
            self.begin(self.value, "ctx", self.bits[0])

    def end_last(self):
        if not self.small:
            return lax.psum(self.value.astype(F32), "ctx")
        return joined(self.value, *self.got, self.at_first, 1).astype(F32)


def meet(sums, *arrays):
    out = list(
        lax.optimization_barrier(sum((item.got for item in sums), ()) + arrays)
    )
    for item in sums:
        item.got, out = tuple(out[: len(item.got)]), out[len(item.got) :]
    return out


def depart(*sums):
    for item, value in zip(sums, lax.optimization_barrier(tuple(item.value for item in sums))):
        item.value = value


def joined(mine, other, place, axis):
    low = jnp.where(place == 0, mine, other)
    high = jnp.where(place == 0, other, mine)
    return jnp.concatenate([low, high], axis=axis)


def stage_weight(me, shards, scratch, sems, start=0):
    rows = scratch.shape[0] // 4
    return [
        pltpu.make_async_copy(
            shard.at[pl.ds(start, rows)], scratch.at[pl.ds(pl.multiple_of((me ^ k) * rows, rows), rows)], sems.at[k]
        )
        for k, shard in enumerate(shards)
    ]


def norm_of(values):
    average = jnp.mean(values, axis=-1, keepdims=True)
    centred = values - average
    inverse = lax.rsqrt(jnp.mean(centred * centred, axis=-1, keepdims=True) + EPS)
    return centred * inverse, inverse


def norm_back(incoming, normal, inverse, gain):
    scaled = incoming * gain
    return inverse * (
        scaled
        - jnp.mean(scaled, axis=-1, keepdims=True)
        - normal * jnp.mean(scaled * normal, axis=-1, keepdims=True)
    )


def head_lanes():
    lane = lax.broadcasted_iota(jnp.int32, (1, PAIR), 1)
    return lane, lane < HEAD


def turned(value, lane):
    ahead = pltpu.roll(value, PAIR - HEAD // 2, 1)
    behind = pltpu.roll(value, HEAD // 2, 1)
    return jnp.where(lane % HEAD < HEAD // 2, ahead, behind)


def stacked(value, first, scale):
    one = jnp.where(first, scale, 0.0).astype(BF16)
    two = jnp.where(first, 0.0, scale).astype(BF16)
    return jnp.concatenate([value * one, value * two], axis=0)


def per_pack(*dims, packs=1):
    return pl.BlockSpec((packs,) + dims, lambda i: (i,) + (0,) * len(dims))


def rows_of(ref):
    return ref[...].reshape(-1, ref.shape[-1])


def put(ref, value):
    ref[...] = value.astype(ref.dtype).reshape(ref.shape)


def fixed(*dims):
    return pl.BlockSpec(dims, lambda i: (0,) * len(dims))


def cost(gflops, megabytes):
    return pl.CostEstimate(
        flops=int(gflops * 1e8), bytes_accessed=int(megabytes * 1e5), transcendentals=0
    )


def ordered(kernel, count, after):
    return lambda *refs: kernel(*refs[:count], *refs[count + len(after) :])


SMEM = pl.BlockSpec(memory_space=pltpu.SMEM)
ANY = pl.BlockSpec(memory_space=pl.ANY)
PARAMS = pltpu.CompilerParams(vmem_limit_bytes=VMEM_BYTES)


def project_kernel(
    me_ref, x_ref, hl_ref, hr_ref, cos_ref, sin_ref, s0, s1, s2, s3,
    q_ref, kv_ref, first_ref, w_ref, gain_ref, sems, gain_sems,
):
    pack = pl.program_id(0)
    block = x_ref.shape[1]
    width = x_ref.shape[2]
    shards = (s0, s1, s2, s3)
    copies = stage_weight(me_ref[0], shards, w_ref, sems)
    gains = [
        pltpu.make_async_copy(
            shard.at[pl.ds(width // 4, 16), pl.ds(0, width)], gain_ref.at[n], gain_sems.at[n]
        )
        for n, shard in enumerate(shards)
    ]

    @pl.when(pack == 0)
    def _():
        for copy in gains + copies:
            copy.start()
        for copy in gains:
            copy.wait()

    values = jnp.concatenate([hl_ref[0], x_ref[0], hr_ref[0]], axis=0).astype(F32)
    normal, _ = norm_of(values)
    gain = jnp.sum(gain_ref[...].astype(F32), axis=0)[:1]
    first_ref[0] = (normal * gain).astype(BF16)
    lane, first = head_lanes()
    cos, sin = cos_ref[...], sin_ref[...]
    own = slice(HALF, HALF + block)
    step = 2 * PAIR

    @pl.when(pack == 0)
    def _():
        for copy in copies:
            copy.wait()

    for j in range(width // step):
        cols = slice(j * step, (j + 1) * step)
        q = dot_nn(first_ref[0, own, :], w_ref[:, cols])
        k = dot_nn(first_ref[0], w_ref[:, width + j * step : width + (j + 1) * step])
        v = dot_nn(first_ref[0], w_ref[:, 2 * width + j * step : 2 * width + (j + 1) * step])
        for i in range(2):
            part = slice(i * PAIR, (i + 1) * PAIR)
            base = j * step + i * PAIR
            qp, kp = q[:, part], k[:, part]
            q_ref[0, :, base : base + PAIR] = (
                qp * cos[own] + turned(qp, lane) * sin[own]
            ).astype(BF16)
            kv_ref[0, :, base : base + PAIR] = (kp * cos + turned(kp, lane) * sin).astype(BF16)
        kv_ref[0, :, width + j * step : width + (j + 1) * step] = v.astype(BF16)


def project(me, tokens, halo_left, halo_right, cos, sin, shards):
    packs, block, width = tokens.shape
    span = block + 2 * HALF
    return pl.pallas_call(
        project_kernel,
        grid=(packs,),
        in_specs=[SMEM, per_pack(block, width), per_pack(HALF, width), per_pack(HALF, width)]
        + [fixed(span, PAIR), fixed(span, PAIR)]
        + [ANY] * 4,
        out_specs=[per_pack(block, width), per_pack(span, 2 * width), per_pack(span, width)],
        out_shape=[
            jax.ShapeDtypeStruct((packs, block, width), BF16),
            jax.ShapeDtypeStruct((packs, span, 2 * width), BF16),
            jax.ShapeDtypeStruct((packs, span, width), BF16),
        ],
        scratch_shapes=[
            pltpu.VMEM((width, 3 * width), BF16),
            pltpu.VMEM((4, 16, width), BF16),
            pltpu.SemaphoreType.DMA((4,)),
            pltpu.SemaphoreType.DMA((4,)),
        ],
        compiler_params=PARAMS,
        cost_estimate=cost(5, 15),
        name="project",
    )(me, tokens, halo_left, halo_right, cos, sin, *shards)


def attend_kernel(left_ok, right_ok, q_ref, kv_ref, probs_ref, mixed_ref):
    pack = pl.program_id(0)
    block, width = q_ref.shape[1], q_ref.shape[2]
    _, first = head_lanes()
    row = lax.broadcasted_iota(jnp.int32, (QROWS, WIN), 0)
    col = lax.broadcasted_iota(jnp.int32, (QROWS, WIN), 1)
    near = (col >= row) & (col <= row + 2 * HALF)
    blocks = block // QROWS
    biases = []
    for b in range(blocks):
        allowed = near
        if b == 0:
            allowed = allowed & ((col >= HALF) | (left_ok[pack] > 0))
        if b == blocks - 1:
            allowed = allowed & ((col < WIN - HALF) | (right_ok[pack] > 0))
        bias = jnp.where(allowed, 0.0, MASKED)
        biases.append(jnp.concatenate([bias, bias], axis=0))
    rows = lambda b: slice(b * QROWS, (b + 1) * QROWS)
    window = lambda b: slice(b * QROWS, b * QROWS + WIN)
    cols = lambda p: slice(p * PAIR, (p + 1) * PAIR)
    for start in range(0, width // PAIR, 2):
        tiles = [(p, b) for p in range(start, start + 2) for b in range(blocks)]
        scores = [
            dot_nt(
                stacked(q_ref[0, rows(b), cols(p)], first, HEAD ** -0.5),
                kv_ref[0, window(b), cols(p)],
            )
            + biases[b]
            for p, b in tiles
        ]
        tops = [jnp.max(item, axis=-1, keepdims=True) for item in scores]
        powers = [jnp.exp(item - top) for item, top in zip(scores, tops)]
        sums = [1.0 / jnp.sum(item, axis=-1, keepdims=True) for item in powers]
        probs = [(item * one).astype(BF16) for item, one in zip(powers, sums)]
        for (p, b), item in zip(tiles, probs):
            probs_ref[0, p, b] = item
            out = dot_nn(item, kv_ref[0, window(b), width + p * PAIR : width + (p + 1) * PAIR])
            mixed_ref[0, rows(b), cols(p)] = jnp.where(first, out[:QROWS], out[QROWS:]).astype(BF16)


def attend(after, left_ok, right_ok, q, kv):
    packs, block, width = q.shape
    pairs, blocks = width // PAIR, block // QROWS
    return pl.pallas_call(
        ordered(attend_kernel, 4, after),
        grid=(packs,),
        in_specs=[SMEM, SMEM, per_pack(block, width), per_pack(block + 2 * HALF, 2 * width)]
        + [ANY] * len(after),
        out_specs=[per_pack(pairs, blocks, 2 * QROWS, WIN), per_pack(block, width)],
        out_shape=[
            jax.ShapeDtypeStruct((packs, pairs, blocks, 2 * QROWS, WIN), BF16),
            jax.ShapeDtypeStruct((packs, block, width), BF16),
        ],
        compiler_params=PARAMS,
        cost_estimate=cost(10, 15),
        name="attend",
    )(left_ok, right_ok, q, kv, *after)


def hidden_kernel(
    me_ref, x_ref, mixed_ref, up_ref, gain_ref, o0, o1, o2, o3, i0, i1, i2, i3,
    out_ref, second_ref, hidden_ref, ggu_ref, middle_ref,
    wo_ref, wi_ref, wd_ref, sems,
):
    tile = pl.program_id(0)
    ff = wd_ref.shape[0]
    both = (o0, o1, o2, o3)
    copies = [
        stage_weight(me_ref[0], both, wo_ref, sems.at[0]),
        stage_weight(me_ref[0], (i0, i1, i2, i3), wi_ref, sems.at[1]),
        stage_weight(me_ref[0], both, wd_ref, sems.at[2], wo_ref.shape[0] // 4),
    ]

    @pl.when(tile == 0)
    def _():
        for group in copies:
            for copy in group:
                copy.start()
        for copy in copies[0]:
            copy.wait()

    middle = rows_of(x_ref).astype(F32) + dot_nn(rows_of(mixed_ref), wo_ref[...])
    put(middle_ref, middle)
    normal, _ = norm_of(middle)
    second = (normal * gain_ref[...]).astype(BF16)
    put(second_ref, second)
    upstream = rows_of(up_ref)

    @pl.when(tile == 0)
    def _():
        for group in copies[1:]:
            for copy in group:
                copy.wait()

    step = ff
    result = middle
    for j in range(ff // step):
        cols = slice(j * step, (j + 1) * step)
        ups = slice(ff + j * step, ff + (j + 1) * step)
        gate = dot_nn(second, wi_ref[:, cols])
        up = dot_nn(second, wi_ref[:, ups])
        grad_hidden = dot_nt(upstream, wd_ref[cols, :])
        cumulative = 0.5 + 0.5 * lax.erf(gate * (0.5 ** 0.5))
        activated = gate * cumulative
        density = jnp.exp(-0.5 * gate * gate) * (1.0 / math.sqrt(2.0 * math.pi))
        hidden = (activated * up).astype(BF16)
        put(hidden_ref.at[:, :, cols], hidden)
        put(ggu_ref.at[:, :, cols], grad_hidden * up * (cumulative + gate * density))
        put(ggu_ref.at[:, :, ups], grad_hidden * activated)
        result = result + dot_nn(hidden, wd_ref[cols, :])
    put(out_ref, result)


def hidden_layer(me, tokens, mixed, upstream, gain, both_shards, in_shards):
    packs, block, width = tokens.shape
    ff = in_shards[0].shape[1] // 2
    shape = lambda dtype, *dims: jax.ShapeDtypeStruct((packs, block) + dims, dtype)
    return pl.pallas_call(
        hidden_kernel,
        grid=(packs // STEP,),
        in_specs=[SMEM] + [per_pack(block, width, packs=STEP)] * 3 + [fixed(1, width)] + [ANY] * 8,
        out_specs=[
            per_pack(block, width, packs=STEP),
            per_pack(block, width, packs=STEP),
            per_pack(block, ff, packs=STEP),
            per_pack(block, 2 * ff, packs=STEP),
            per_pack(block, width, packs=STEP),
        ],
        out_shape=[
            shape(BF16, width),
            shape(BF16, width),
            shape(BF16, ff),
            shape(BF16, 2 * ff),
            shape(BF16, width),
        ],
        scratch_shapes=[
            pltpu.VMEM((width, width), BF16),
            pltpu.VMEM((width, 2 * ff), BF16),
            pltpu.VMEM((ff, width), BF16),
            pltpu.SemaphoreType.DMA((3, 4)),
        ],
        compiler_params=PARAMS,
        cost_estimate=cost(16, 25),
        name="hidden_layer",
    )(me, tokens, mixed, upstream, gain, *both_shards, *in_shards)


def middle_kernel(
    me_ref, middle_ref, ggu_ref, up_ref, mixed_ref, gain_ref, o0, o1, o2, o3, i0, i1, i2, i3,
    low_ref, gmix_ref, gout_ref, wo_ref, wi_ref, total_ref, sems,
):
    tile = pl.program_id(0)
    copies = [
        stage_weight(me_ref[0], group, scratch, sems.at[n])
        for n, (group, scratch) in enumerate(
            (((o0, o1, o2, o3), wo_ref), ((i0, i1, i2, i3), wi_ref))
        )
    ]

    @pl.when(tile == 0)
    def _():
        for group in copies:
            for copy in group:
                copy.start()
        total_ref[...] = jnp.zeros_like(total_ref)

    normal, inverse = norm_of(rows_of(middle_ref).astype(F32))

    @pl.when(tile == 0)
    def _():
        for group in copies:
            for copy in group:
                copy.wait()

    grad_second = dot_nt(rows_of(ggu_ref), wi_ref[...])
    grad_middle = rows_of(up_ref).astype(F32) + norm_back(grad_second, normal, inverse, gain_ref[...])
    low = grad_middle.astype(BF16)
    put(low_ref, low)
    put(gmix_ref, dot_nt(low, wo_ref[...]))
    total_ref[...] += dot_tn(rows_of(mixed_ref), low)

    @pl.when(tile == pl.num_programs(0) - 1)
    def _():
        gout_ref[...] = total_ref[...].astype(BF16)


def middle_back(after, me, middle, ggu, upstream, mixed, gain, out_shards, in_shards):
    packs, block, width = middle.shape
    wide = ggu.shape[2]
    shape = lambda dtype, *dims: jax.ShapeDtypeStruct((packs, block) + dims, dtype)
    return pl.pallas_call(
        ordered(middle_kernel, 14, after),
        grid=(packs // STEP,),
        in_specs=[SMEM, per_pack(block, width, packs=STEP), per_pack(block, wide, packs=STEP)]
        + [per_pack(block, width, packs=STEP)] * 2
        + [fixed(1, width)]
        + [ANY] * (8 + len(after)),
        out_specs=[per_pack(block, width, packs=STEP)] * 2 + [fixed(width, width)],
        out_shape=[
            shape(BF16, width),
            shape(BF16, width),
            jax.ShapeDtypeStruct((width, width), BF16),
        ],
        scratch_shapes=[
            pltpu.VMEM((width, width), BF16),
            pltpu.VMEM((width, wide), BF16),
            pltpu.VMEM((width, width), F32),
            pltpu.SemaphoreType.DMA((2, 4)),
        ],
        compiler_params=PARAMS,
        cost_estimate=cost(8, 20),
        name="middle_back",
    )(me, middle, ggu, upstream, mixed, gain, *out_shards, *in_shards, *after)


GROUP = 3 * PAIR


def attend_back_kernel(
    me_ref, q_ref, k_ref, v_ref, probs_ref, gmix_ref, cos_ref, sin_ref, first_ref,
    dqkv_ref, grad_ref, all_ref,
):
    block = q_ref.shape[1]
    lane, first = head_lanes()
    cos, sin = cos_ref[...], -sin_ref[...]
    own = slice(HALF, HALF + block)
    dqkv_ref[0, :HALF, :GROUP] = jnp.zeros((HALF, GROUP), BF16)
    dqkv_ref[0, HALF + block :, :GROUP] = jnp.zeros((HALF, GROUP), BF16)
    tiles = [(p, b) for p in range(GROUP // PAIR) for b in range(block // QROWS)]
    rows = lambda b: slice(b * QROWS, (b + 1) * QROWS)
    window = lambda b: slice(b * QROWS, b * QROWS + WIN)
    cols = lambda p: slice(p * PAIR, (p + 1) * PAIR)
    do2 = [stacked(gmix_ref[0, rows(b), cols(p)], first, 1.0) for p, b in tiles]
    q2 = [stacked(q_ref[0, rows(b), cols(p)], first, HEAD ** -0.5) for p, b in tiles]
    dprobs = [dot_nt(do, v_ref[0, window(b), cols(p)]) for do, (p, b) in zip(do2, tiles)]
    dvs = [dot_tn(probs_ref[0, p, b], do) for do, (p, b) in zip(do2, tiles)]
    wide = [probs_ref[0, p, b].astype(F32) for p, b in tiles]
    inner = [jnp.sum(d * w, axis=-1, keepdims=True) for d, w in zip(dprobs, wide)]
    ds = [(w * (d - i)).astype(BF16) for w, d, i in zip(wide, dprobs, inner)]
    dq2 = [dot_nn(d, k_ref[0, window(b), cols(p)]) for d, (p, b) in zip(ds, tiles)]
    dqs = [jnp.where(first, d[:QROWS], d[QROWS:]) * (HEAD ** -0.5) for d in dq2]
    dks = [dot_tn(d, q) for d, q in zip(ds, q2)]
    over = WIN - QROWS
    merge = lambda a, b: jnp.concatenate([a[:QROWS], a[QROWS:] + b[:over], b[over:]], axis=0)
    for p in range(GROUP // PAIR):
        dq = jnp.concatenate(dqs[2 * p : 2 * p + 2], axis=0)
        dk, dv = merge(*dks[2 * p : 2 * p + 2]), merge(*dvs[2 * p : 2 * p + 2])
        at = lambda n: slice(n * GROUP + p * PAIR, n * GROUP + (p + 1) * PAIR)
        dqkv_ref[0, own, at(0)] = (dq * cos[own] + turned(dq, lane) * sin[own]).astype(BF16)
        dqkv_ref[0, :, at(1)] = (dk * cos + turned(dk, lane) * sin).astype(BF16)
        dqkv_ref[0, :, at(2)] = dv.astype(BF16)
    all_ref[pl.program_id(0)] = dqkv_ref[0]

    @pl.when(pl.program_id(0) == pl.num_programs(0) - 1)
    def _():
        for n in range(3):
            part = slice(n * GROUP, (n + 1) * GROUP)
            right = all_ref[:, :, part].reshape(-1, GROUP)
            grad_ref[:, part] = dot_tn(rows_of(first_ref), right).astype(BF16)


def attend_back(group, after, me, q, kv, probs, gmix, cos, sin, first_in):
    packs, block, width = q.shape
    span = block + 2 * HALF
    blocks, groups = block // QROWS, width // GROUP
    cols = lambda rows, g: pl.BlockSpec((1, rows, GROUP), lambda i: (i, 0, g))
    return pl.pallas_call(
        ordered(attend_back_kernel, 9, after),
        grid=(packs,),
        in_specs=[
            SMEM,
            cols(block, group),
            cols(span, group),
            cols(span, groups + group),
            pl.BlockSpec(
                (1, GROUP // PAIR, blocks, 2 * QROWS, WIN), lambda i: (i, group, 0, 0, 0)
            ),
            cols(block, group),
            fixed(span, PAIR),
            fixed(span, PAIR),
            fixed(packs, span, width),
        ]
        + [ANY] * len(after),
        out_specs=[per_pack(span, 3 * GROUP), fixed(width, 3 * GROUP)],
        out_shape=[
            jax.ShapeDtypeStruct((packs, span, 3 * GROUP), BF16),
            jax.ShapeDtypeStruct((width, 3 * GROUP), BF16),
        ],
        scratch_shapes=[pltpu.VMEM((packs, span, 3 * GROUP), BF16)],
        compiler_params=PARAMS,
        cost_estimate=cost(8, 10),
        name="attend_back",
    )(me, q, kv, kv, probs, gmix, cos, sin, first_in, *after)


def halo_back_kernel(
    me_ref, l0, l1, r0, r1, s0, s1, s2, s3, left_ref, right_ref, w_ref, sems
):
    copies = stage_weight(me_ref[0], (s0, s1, s2, s3), w_ref, sems)
    width = left_ref.shape[2]

    @pl.when(pl.program_id(0) == 0)
    def _():
        for copy in copies:
            copy.start()
        for copy in copies:
            copy.wait()

    parts = [
        jnp.concatenate([rows_of(left)[:, GROUP:], rows_of(right)[:, GROUP:]], axis=0)
        for left, right in ((l0, r0), (l1, r1))
    ]
    rows = jnp.concatenate(
        [part[:, n * GROUP : (n + 1) * GROUP] for n in range(2) for part in parts], axis=1
    )
    grads = dot_nt(rows, w_ref[:, width:])
    half = grads.shape[0] // 2
    put(left_ref, grads[:half])
    put(right_ref, grads[half:])


def halo_back(after, me, parts, shards):
    packs, span, _ = parts[0].shape
    width = shards[0].shape[1] // 3
    edge = lambda n: pl.BlockSpec((packs, HALF, 3 * GROUP), lambda i: (i, n, 0))
    return pl.pallas_call(
        ordered(halo_back_kernel, 9, after),
        grid=(1,),
        in_specs=[SMEM] + [edge(0)] * 2 + [edge(span // HALF - 1)] * 2
        + [ANY] * (4 + len(after)),
        out_specs=[per_pack(HALF, width, packs=packs)] * 2,
        out_shape=[jax.ShapeDtypeStruct((packs, HALF, width), BF16)] * 2,
        scratch_shapes=[pltpu.VMEM((width, 3 * width), BF16), pltpu.SemaphoreType.DMA((4,))],
        compiler_params=PARAMS,
        cost_estimate=cost(1.2, 6),
        name="halo_back",
    )(me, *parts, *parts, *shards, *after)


def own_back_kernel(me_ref, p0, p1, s0, s1, s2, s3, own_ref, w_ref, sems):
    copies = stage_weight(me_ref[0], (s0, s1, s2, s3), w_ref, sems)
    block = own_ref.shape[1]

    @pl.when(pl.program_id(0) == 0)
    def _():
        for copy in copies:
            copy.start()
        for copy in copies:
            copy.wait()

    own = slice(HALF, HALF + block)
    parts = [part[:, own, :].reshape(-1, part.shape[2]) for part in (p0, p1)]
    rows = jnp.concatenate(
        [part[:, n * GROUP : (n + 1) * GROUP] for n in range(3) for part in parts], axis=1
    )
    put(own_ref, dot_nt(rows, w_ref[...]))


def own_back(after, me, parts, shards):
    packs, span, _ = parts[0].shape
    block, width = span - 2 * HALF, shards[0].shape[1] // 3
    return pl.pallas_call(
        ordered(own_back_kernel, 7, after),
        grid=(packs // STEP,),
        in_specs=[SMEM] + [per_pack(span, 3 * GROUP, packs=STEP)] * 2
        + [ANY] * (4 + len(after)),
        out_specs=per_pack(block, width, packs=STEP),
        out_shape=jax.ShapeDtypeStruct((packs, block, width), BF16),
        scratch_shapes=[pltpu.VMEM((width, 3 * width), BF16), pltpu.SemaphoreType.DMA((4,))],
        compiler_params=PARAMS,
        cost_estimate=cost(5, 15),
        name="own_back",
    )(me, *parts, *shards, *after)


def finish_kernel(x_ref, own_ref, fl_ref, fr_ref, gm_ref, gain_ref, out_ref):
    block = x_ref.shape[1]
    normal, inverse = norm_of(x_ref[0].astype(F32))
    grad = own_ref[0].astype(F32)
    grad = jnp.concatenate(
        [
            grad[:HALF] + fl_ref[0].astype(F32),
            grad[HALF : block - HALF],
            grad[block - HALF :] + fr_ref[0].astype(F32),
        ],
        axis=0,
    )
    out_ref[0] = (gm_ref[0] + norm_back(grad, normal, inverse, gain_ref[...])).astype(BF16)


def finish(after, tokens, own, from_left, from_right, grad_middle, gain):
    packs, block, width = tokens.shape
    per_pack = lambda *dims: pl.BlockSpec((1,) + dims, lambda i: (i,) + (0,) * len(dims))
    return pl.pallas_call(
        ordered(finish_kernel, 6, after),
        grid=(packs,),
        in_specs=[
            per_pack(block, width),
            per_pack(block, width),
            per_pack(HALF, width),
            per_pack(HALF, width),
            per_pack(block, width),
            pl.BlockSpec((1, width), lambda i: (0, 0)),
        ]
        + [ANY] * len(after),
        out_specs=per_pack(block, width),
        out_shape=jax.ShapeDtypeStruct((packs, block, width), BF16),
        cost_estimate=pl.CostEstimate(flops=20_000_000, bytes_accessed=10_000_000, transcendentals=0),
        name="finish",
    )(tokens, own, from_left, from_right, grad_middle, gain, *after)


def tables(start, count):
    half_size = HEAD // 2
    freqs = jnp.power(THETA, -jnp.arange(half_size, dtype=F32) * (2.0 / HEAD))
    positions = (start + jnp.arange(count, dtype=jnp.int32)).astype(F32)
    angles = positions[:, None] * freqs[None, :]
    cos, sin = jnp.cos(angles), jnp.sin(angles)
    return (
        jnp.concatenate([cos, cos, cos, cos], axis=-1),
        jnp.concatenate([-sin, sin, -sin, sin], axis=-1),
    )


def weight_grad(left, right):
    return dot_tn(
        left.reshape(-1, left.shape[-1]), right.reshape(-1, right.shape[-1])
    ).astype(BF16)


def gain_grad(grad, weight, gain):
    return jnp.sum(grad * weight.astype(F32), axis=1) / gain.astype(F32)


def per_device(tokens, doc_begin, gain_attn, w_qkv, w_att_out, gain_mlp, w_in, w_down, cotangent):
    packs, block, width = tokens.shape
    me_w, me_c = lax.axis_index("wsh"), lax.axis_index("ctx")
    me = me_w.reshape(1).astype(jnp.int32)
    part = gain_attn.shape[0]

    row = jnp.zeros((16, w_qkv.shape[1]), BF16)
    row = lax.dynamic_update_slice(row, gain_attn[None], (0, me_w * part))
    row = lax.dynamic_update_slice(row, gain_mlp[None], (0, width + me_w * part))
    qkv = jnp.concatenate([w_qkv, row], axis=0)
    qkv_near, qkv_far = swap(qkv, "wsh", 1), swap(qkv, "wsh", 2)
    halo_left = shifted(tokens[:, block - HALF :], "ctx", 1)
    doc_rows = jnp.broadcast_to(doc_begin.astype(BF16)[:, :, None], (packs, 16, width))
    halo_right = shifted(jnp.concatenate([tokens[:, :HALF], doc_rows], axis=1), "ctx", -1)
    both = jnp.concatenate([w_att_out, w_down], axis=0)
    at_x, half_rows = me_c % 2, part // 2
    in_half = lax.dynamic_slice_in_dim(w_in, at_x * half_rows, half_rows, 0)
    qkv_far, halo_left, halo_right, in_half, both = lax.optimization_barrier(
        (qkv_far, halo_left, halo_right, in_half, both)
    )
    in_half = swap(in_half, "wsh", 2)
    both_far = swap(both, "wsh", 2)
    qkv_shards = (qkv, qkv_near, qkv_far, swap(qkv_far, "wsh", 1))
    gain_rows = sum(shard[part : part + 1].astype(F32) for shard in qkv_shards)
    gain_one, gain_two = gain_rows[:, :width], gain_rows[:, width : 2 * width]
    doc_right = halo_right[:, HALF, 0].astype(jnp.int32)
    left_ok = (doc_begin[:, 0] < me_c).astype(jnp.int32)
    right_ok = (
        (doc_right == doc_begin[:, 0]) & (me_c + 1 < lax.axis_size("ctx"))
    ).astype(jnp.int32)
    cos, sin = tables(me_c * block - HALF, block + 2 * HALF)


    q, kv, first_in = project(
        me, tokens, halo_left, halo_right, cos, sin, qkv_shards
    )
    in_half, q = lax.optimization_barrier((in_half, q))
    in_other = swap(in_half, "ctx", 1)
    both_near, in_near = swap(both, "wsh", 1), swap(w_in, "wsh", 1)
    probs, mixed = attend((), left_ok, right_ok, q, kv)
    both_far, in_half, in_other, both_near, in_near, mixed = lax.optimization_barrier(
        (both_far, in_half, in_other, both_near, in_near, mixed)
    )
    both_far_near = swap(both_far, "wsh", 1)
    in_far = joined(in_half, in_other, at_x, 0)
    in_far_near = swap(in_far, "wsh", 1)
    in_shards = (w_in, in_near, in_far, in_far_near)
    both_shards = (both, both_near, both_far, both_far_near)

    output, second_in, hidden, ggu, middle = hidden_layer(
        me, tokens, mixed, cotangent, gain_two, both_shards, in_shards
    )
    grad = weight_grad(second_in, ggu)
    sum_in = Reduction(grad, bits=(2, 1))
    sum_in.value, hidden = lax.optimization_barrier((sum_in.value, hidden))
    sum_in.begin_core()
    sum_both = Reduction(weight_grad(hidden, cotangent), bits=(2, 1))
    (sum_both.value,) = meet((sum_in,), sum_both.value)
    sum_in.end_core()
    sum_in.begin_side()
    sum_both.begin_core()
    low, gmix, grad_out = middle_back(
        (sum_in.value, sum_both.value),
        me, middle, ggu, cotangent, mixed, gain_two, both_shards, in_shards,
    )
    low, gmix, grad_out = meet((sum_both, sum_in), low, gmix, grad_out)
    sum_both.end_core()
    sum_in.end_side()
    sum_out = Reduction(grad_out)
    sum_out.begin_core()
    sum_out.end_core()
    sum_both.join(sum_out)
    depart(sum_in, sum_both)
    sum_both.begin_side()
    sum_in.begin_plane()
    back = lambda group, *after: attend_back(
        group, after, me, q, kv, probs, gmix, cos, sin, first_in
    )
    back_0, grad_0 = back(0, sum_in.value, sum_both.value)
    back_0, grad_0 = meet((sum_in, sum_both), back_0, grad_0)
    sum_in.end_plane()
    sum_both.end_side()
    sum_0 = Reduction(grad_0)
    sum_0.begin_core()
    sum_0.end_core()
    depart(sum_in, sum_both, sum_0)
    sum_0.begin_side()
    sum_in.begin_far()
    sum_both.begin_across()
    back_1, grad_1 = back(1, sum_in.value, sum_both.value, sum_0.value)
    back_1, grad_1 = meet((sum_in, sum_both, sum_0), back_1, grad_1)
    sum_in.end_far()
    sum_both.end_across()
    sum_0.end_side()
    sum_1 = Reduction(grad_1)
    sum_1.begin_core()
    depart(sum_in, sum_both, sum_0)
    sum_in.begin_spread()
    sum_1.end_core()
    sum_1.begin_side()
    sum_0.begin_across()
    sum_both.begin_near()
    parts = (back_0, back_1)
    to_left, to_right = halo_back(
        (sum_1.value, sum_in.value, sum_0.value, sum_both.value), me, parts, qkv_shards
    )
    to_left, to_right = meet((sum_0, sum_both, sum_in), to_left, to_right)
    sum_0.end_across()
    sum_both.end_near()
    sum_in.end_spread()
    depart(sum_0, sum_both, sum_in)
    sum_in.begin_last()
    sum_0.begin_near()
    from_right = shifted(to_left, "ctx", -1)
    from_left = shifted(to_right, "ctx", 1)
    own = own_back((sum_0.value, sum_both.value), me, parts, qkv_shards)
    own, from_left, from_right = meet((sum_0, sum_1, sum_in), own, from_left, from_right)
    sum_1.end_side()
    sum_0.end_near()
    depart(sum_0, sum_1, sum_both)
    sum_1.begin_plane()
    sum_0.begin_far()
    sum_both.begin_far()
    grad_tokens = finish(
        (sum_1.value, sum_0.value, sum_both.value),
        tokens, own, from_left, from_right, low, gain_one,
    )
    (grad_tokens,) = meet((sum_0, sum_1, sum_both), grad_tokens)
    sum_1.end_plane()
    sum_0.end_far()
    sum_both.end_far()
    depart(sum_0, sum_1, sum_both)
    sum_1.begin_far()
    sum_0.begin_spread()
    sum_both.begin_spread()
    meet((sum_0, sum_1, sum_both))
    sum_1.end_far()
    sum_0.end_spread()
    sum_both.end_spread()
    depart(sum_0, sum_1, sum_both)
    sum_1.begin_gather()
    sum_0.begin_last()
    sum_both.begin_last()
    meet((sum_0, sum_1, sum_both))
    grad_in = sum_in.end_last()
    grad_both = sum_both.end_last()
    pieces = [sum_0.end_last(), sum_1.end_gather()]
    grad_qkv = jnp.concatenate(
        [item[:, n * GROUP : (n + 1) * GROUP] for n in range(3) for item in pieces], axis=1
    )
    down = w_down.shape[0]
    return (
        output, grad_tokens, gain_grad(grad_qkv, w_qkv, gain_attn), grad_qkv, grad_both[down:],
        gain_grad(grad_in, w_in, gain_mlp), grad_in, grad_both[:down],
    )


def solution(mesh):
    return jax.shard_map(
        per_device,
        mesh=mesh,
        in_specs=(
            P("wsh", "ctx", None),
            P("wsh", "ctx"),
            P("wsh"),
            P("wsh", None),
            P("wsh", None),
            P("wsh"),
            P("wsh", None),
            P("wsh", None),
            P("wsh", "ctx", None),
        ),
        out_specs=(
            P("wsh", "ctx", None),
            P("wsh", "ctx", None),
            P("wsh"),
            P("wsh", None),
            P("wsh", None),
            P("wsh"),
            P("wsh", None),
            P("wsh", None),
        ),
        check_vma=False,
    )
```
